256 devices in a mesh: wedge: 64 (over x_lo, z, y), band: 4 (over x_hi, core).
Axes of the slice: x: 4 (x_hi: 2, x_lo: 2; x = x_hi * 2 + x_lo), y: 4, z: 8, core: 2. Of those that a mesh axis runs over, the one named last changes fastest.
Arguments:
- pulse_data: bfloat16 [2, 1024, 4096], P(None, 'wedge', 'band'), may hold values from -6 to 6
- phase_error: float32 [1024], P('wedge'), may hold values from -3.140625 to 3.140625
- steering: bfloat16 [2, 4096, 1024], P(None, 'wedge'), may hold values from -0.1875 to 0.1875
- kernel_bank: bfloat16 [8, 128, 4096], P(None, None, 'band'), may hold values from -0.25 to 0.25
- tile_offsets: int32 [64, 64, 4], replicated, may hold values from 0 to 7, as said below
- kernel_ids: int32 [64, 64, 4], replicated, may hold values from 0 to 7
- counts: int32 [64, 64], replicated, may hold values from 0 to 4, as said below
Outputs:
- focused: float32 [2, 4096, 4096], P(None, 'wedge', 'band')
- smoothed: float32 [2, 4096, 4096], P(None, 'wedge', 'band')
- phase_gradient: float32 [1024], P('wedge')
The draws below stay inside these ranges and needn't reach their ends.
Inputs may be any that keep to these rules, and one draw needn't show every extreme that they name: counts[k, w] is the number of live slots of pulse block k at wedge w; 4 is reached. `tile_offsets`: the 4 tiles named for one pair are distinct; only the first counts[k, w] of them are used.
All inputs are finite; a program needn't handle non-finite values.
Results may differ from the reference program's by a relative error of at most 0.006.
Values may be sent and summed in bfloat16 or wider, within the bound.
A program may use at most 64 MiB of HBM per device.

```python
import math
import jax
import jax.numpy as jnp
from jax import lax

PULSE_DEV = 16
AZ_DEV = 64
RB_DEV = 1024
RANGE_DEV = 1024
TILE = 128
MAXB = 4
KERNELS = 8
BLOCKS = 64
PULSES = 1024
AZIMUTH = 4096
RADIAL = 4096
RANGE = 4096
NTILES = 8
N_WEDGE = 64
N_BAND = 4


def draw_counts(key, part):
    key = jax.random.fold_in(key, 11)
    first_key, second_key, third_key, fourth_key = jax.random.split(key, 4)
    ceiling = jax.random.randint(first_key, (1, BLOCKS), 1, MAXB + 1)
    drawn = jax.random.randint(second_key, (BLOCKS, BLOCKS), 0, ceiling + 1)
    chosen_row = jax.random.randint(third_key, (), 0, BLOCKS)
    chosen_col = jax.random.randint(fourth_key, (), 0, BLOCKS)
    rows_grid = jnp.arange(BLOCKS, dtype=jnp.int32)[:, None]
    cols_grid = jnp.arange(BLOCKS, dtype=jnp.int32)[None, :]
    marked = (rows_grid == chosen_row) & (cols_grid == chosen_col)
    return jnp.where(marked, MAXB, drawn).astype(jnp.int32)


def draw_tile_offsets(key, part):
    key = jax.random.fold_in(key, 23)
    scores = jax.random.randint(key, (BLOCKS, BLOCKS, NTILES), 0, 1048576) * NTILES + jnp.arange(NTILES, dtype=jnp.int32)
    order = jnp.argsort(scores, axis=2, stable=True)
    return order[:, :, :MAXB].astype(jnp.int32)


def touch_ends(values, key, smallest, top_value):
    extent = values.shape
    index_at = [jax.random.randint(jax.random.fold_in(key, axis), (), 0, extent[axis]) for axis in range(len(extent))]
    values = values.at[tuple(index_at)].set(smallest)
    longest = extent.index(max(extent))
    index_at[longest] = (index_at[longest] + 1) % extent[longest]
    return values.at[tuple(index_at)].set(top_value)


def shard_levels(key, extent, cuts, low, top_value):
    factor_of = 1.0
    for axis_at, blocks in cuts:
        steps = jax.random.uniform(jax.random.fold_in(jax.random.fold_in(key, 6), axis_at), (blocks,), jnp.float32, low / len(cuts), top_value / len(cuts))
        factor_of = factor_of * jnp.repeat(jnp.exp(steps), extent[axis_at] // blocks).reshape((-1,) + (1,) * (len(extent) - 1 - axis_at))
    return factor_of


def bell_draw(rng, extent, scale, limit, shards=(), kind=jnp.bfloat16):
    level = shard_levels(rng, extent, shards, -0.22, 0.18) if shards else 1.0
    values = jax.random.normal(rng, extent, jnp.float32) * scale * level
    return jnp.minimum(jnp.maximum(values, -limit), limit).astype(kind)


def setup_inputs(seed: int = 0) -> dict:
    key_of = jax.random.split(jax.random.key(seed), 8)
    pulse_data = bell_draw(key_of[0], (2, PULSES, RANGE), 1.0, 6.0, ((1, 64), (2, 4)))
    phase_error = jnp.clip(jax.random.uniform(key_of[1], (PULSES,), jnp.float32, -3.140625, 3.140625), -3.140625, 3.140625)
    steering = bell_draw(key_of[2], (2, AZIMUTH, PULSES), PULSES ** -0.5, 0.1875, ((1, 64),))
    kernel_bank = bell_draw(key_of[3], (KERNELS, TILE, RADIAL), (4 * TILE) ** -0.5, 0.25, ((2, 4),))
    tile_offsets = draw_tile_offsets(jax.random.fold_in(key_of[7], 71), 0)
    kernel_ids = touch_ends(jax.random.randint(key_of[5], (BLOCKS, BLOCKS, MAXB), 0, KERNELS), jax.random.fold_in(key_of[5], 1), 0, KERNELS - 1).astype(jnp.int32)
    counts = draw_counts(jax.random.fold_in(key_of[7], 71), 0)
    return {"pulse_data": pulse_data, "phase_error": phase_error, "steering": steering, "kernel_bank": kernel_bank, "tile_offsets": tile_offsets, "kernel_ids": kernel_ids, "counts": counts}


EDGE_SOFTNESS = 0.05
STEP_SIZE = 0.25

def correct_phase(pulse_data, phase_error):
    cosine = jnp.cos(phase_error)[:, None]
    sine_part = jnp.sin(phase_error)[:, None]
    real_part = pulse_data[0].astype(jnp.float32)
    imag_part = pulse_data[1].astype(jnp.float32)
    corrected = jnp.stack([real_part * cosine + imag_part * sine_part, imag_part * cosine - real_part * sine_part])
    return corrected.astype(jnp.bfloat16)

def resample_pair(pulse_block, bank_band, offsets, kernels, count):
    pulse_rows = pulse_block.shape[1]
    radial_cells = bank_band.shape[2]
    pieces = [lax.dynamic_slice_in_dim(pulse_block, offsets[slot_index] * TILE, TILE, 2) for slot_index in range(MAXB)]
    joined = jnp.reshape(jnp.concatenate(pieces, axis=2), (2 * pulse_rows, MAXB * TILE))
    live = (jnp.arange(MAXB) < count).astype(bank_band.dtype)
    chosen = jnp.take(bank_band, kernels, axis=0) * live[:, None, None]
    running = jnp.dot(joined, jnp.reshape(chosen, (MAXB * TILE, radial_cells)), preferred_element_type=jnp.float32)
    return jnp.reshape(running, (2, pulse_rows, radial_cells)).astype(jnp.bfloat16)

def image_and_partial(resampled, steering_rows):
    pulse_total = resampled.shape[1]
    radial_cells = resampled.shape[2]
    azimuth_rows = steering_rows.shape[1]
    stacked_rows = jnp.reshape(resampled, (2 * pulse_total, radial_cells))
    left_real = jnp.concatenate([steering_rows[0], -steering_rows[1]], axis=1)
    left_imag = jnp.concatenate([steering_rows[1], steering_rows[0]], axis=1)
    focus_real = jnp.dot(left_real, stacked_rows, preferred_element_type=jnp.float32)
    focus_imag = jnp.dot(left_imag, stacked_rows, preferred_element_type=jnp.float32)
    squared = focus_real * focus_real + focus_imag * focus_imag
    cubed = jnp.stack([squared * focus_real, squared * focus_imag]).astype(jnp.bfloat16)
    cubed_rows = jnp.reshape(cubed, (2 * azimuth_rows, radial_cells))
    right_real = jnp.reshape(steering_rows, (2 * azimuth_rows, pulse_total))
    right_imag = jnp.concatenate([steering_rows[1], -steering_rows[0]], axis=0)
    contract = (((0,), (0,)), ((), ()))
    back_real = lax.dot_general(right_real, cubed_rows, contract, preferred_element_type=jnp.float32)
    back_imag = lax.dot_general(right_imag, cubed_rows, contract, preferred_element_type=jnp.float32)
    partial_sum = lax.optimization_barrier(jnp.sum(back_real * resampled[1].astype(jnp.float32) + back_imag * resampled[0].astype(jnp.float32), axis=1))
    return (jnp.stack([focus_real, focus_imag]), partial_sum)

def edge_pull(difference):
    return difference / jnp.sqrt(lax.optimization_barrier(jnp.sum(difference * difference, axis=0, keepdims=True)) + EDGE_SOFTNESS)

def reference(pulse_data, phase_error, steering, kernel_bank, tile_offsets, kernel_ids, counts):
    corrected = correct_phase(pulse_data, phase_error)

    def tile_for(position):
        wedge_index = position // N_BAND
        band_index = position % N_BAND
        corrected_band = lax.dynamic_slice_in_dim(corrected, band_index * RANGE_DEV, RANGE_DEV, 2)
        bank_band = lax.dynamic_slice_in_dim(kernel_bank, band_index * RB_DEV, RB_DEV, 2)
        steering_rows = lax.dynamic_slice_in_dim(steering, wedge_index * AZ_DEV, AZ_DEV, 1)
        offsets_wedge = lax.dynamic_index_in_dim(tile_offsets, wedge_index, 1, keepdims=False)
        kernels_wedge = lax.dynamic_index_in_dim(kernel_ids, wedge_index, 1, keepdims=False)
        counts_wedge = lax.dynamic_index_in_dim(counts, wedge_index, 1, keepdims=False)

        def for_block(block_index):
            pulse_block = lax.dynamic_slice_in_dim(corrected_band, block_index * PULSE_DEV, PULSE_DEV, 1)
            return resample_pair(pulse_block, bank_band, offsets_wedge[block_index], kernels_wedge[block_index], counts_wedge[block_index])
        blocks = lax.map(for_block, jnp.arange(BLOCKS).astype(jnp.int32))
        resampled = jnp.reshape(jnp.moveaxis(blocks, 0, 1), (2, PULSES, RB_DEV))
        return image_and_partial(resampled, steering_rows)
    tiles, partial_sums = lax.map(tile_for, jnp.arange(N_WEDGE * N_BAND).astype(jnp.int32))
    grouped = jnp.reshape(tiles, (N_WEDGE, N_BAND, 2, AZ_DEV, RB_DEV))
    focused = jnp.reshape(jnp.transpose(grouped, (2, 0, 3, 1, 4)), (2, AZIMUTH, RADIAL))
    phase_gradient = math.sqrt(PULSES / (AZIMUTH * RADIAL)) * lax.optimization_barrier(jnp.sum(partial_sums, axis=0))
    padded = jnp.pad(focused, ((0, 0), (0, 0), (1, 1)))
    columns = jnp.arange(RADIAL)
    lower_valid = (columns > 0)[None, None, :]
    upper_valid = (columns < RADIAL - 1)[None, None, :]
    summed = edge_pull(focused - jnp.roll(focused, 1, axis=1)) + edge_pull(focused - jnp.roll(focused, -1, axis=1))
    summed = summed + jnp.where(lower_valid, edge_pull(focused - padded[:, :, :-2]), 0.0)
    summed = summed + jnp.where(upper_valid, edge_pull(focused - padded[:, :, 2:]), 0.0)
    smoothed = focused - STEP_SIZE * summed
    return (focused, smoothed, phase_gradient)
```

```python
import functools
import math

import jax
import jax.numpy as jnp
from jax import lax
from jax.experimental import pallas as pl
from jax.experimental.pallas import tpu as pltpu
from jax.sharding import PartitionSpec as P

TILE = 128
MAXB = 4
EDGE_SOFTNESS = 0.05
STEP_SIZE = 0.25
XN, ZN, YN, BN = 2, 8, 4, 4
MESH = pl.DeviceIdType.MESH
COPIES = 192


def kernel(scale, table, phase, pulses, steering, bank, focused_out, smoothed_out, gradient_out, *scratch):
    scratch = list(scratch)
    take = lambda n: [scratch.pop(0) for _ in range(n)]
    own0, pair0, own1 = take(ZN), take(ZN), take(ZN)
    column1 = take(ZN)
    y_send, y_got = take(ZN), take(ZN)
    x_send, x_got = take(ZN), take(ZN)
    lhs, resampled, bank_v, steer_v, image, smooth = take(6)
    rows_send, rows_got, cols_send, cols_got = take(4)
    part_one, got_one, part_two, got_two = take(4)
    send_sem, recv_sem, load_sem = take(3)

    w = lax.axis_index("wedge")
    b = lax.axis_index("band")
    x, z, y = w // (ZN * YN), lax.rem(w // YN, ZN), lax.rem(w, YN)

    def at(dx, dz, dy):
        return lax.rem(x + dx, XN) * (ZN * YN) + lax.rem(z + dz, ZN) * YN + lax.rem(y + dy, YN)

    loads = [
        pltpu.make_async_copy(bank, bank_v, load_sem.at[0]),
        pltpu.make_async_copy(steering, steer_v, load_sem.at[1]),
    ]
    for load in loads:
        load.start()

    greeted = [(at(0, dz, 0), b) for dz in range(1, ZN)]
    plane = [
        (dx, dy, db) for db in range(BN) for dx in range(XN) for dy in range(YN) if (dx, dy, db) != (0, 0, 0)
    ]
    greeted += [(at(dx, 0, dy), lax.rem(b + db, BN)) for dx, dy, db in plane]
    wedges = XN * ZN * YN
    after, before = lax.rem(w + 1, wedges), lax.rem(w + wedges - 1, wedges)
    greeted += [(after, b), (before, b)]
    barrier = pltpu.get_barrier_semaphore()
    for device in greeted:
        pl.semaphore_signal(barrier, inc=1, device_id=device, device_id_type=MESH)

    square = lax.broadcasted_iota(jnp.int32, (16, 16), 0) == lax.broadcasted_iota(jnp.int32, (16, 16), 1)
    angle = jnp.sum(jnp.where(square, phase[...], 0.0), axis=1, keepdims=True)
    cosine, sine = jnp.cos(angle), jnp.sin(angle)
    real, imag = pulses[0].astype(jnp.float32), pulses[1].astype(jnp.float32)
    fixed0 = (real * cosine + imag * sine).astype(jnp.bfloat16)
    fixed1 = (imag * cosine - real * sine).astype(jnp.bfloat16)
    for t in range(8):
        own0[0][t] = fixed0[:, t * TILE : (t + 1) * TILE]
        own1[0][t] = fixed1[:, t * TILE : (t + 1) * TILE]

    pl.semaphore_wait(barrier, len(greeted))

    started = []

    def copy(src, dst, device):
        index = len(started)
        made = pltpu.make_async_remote_copy(
            src, dst, send_sem.at[index], recv_sem.at[index], device_id=device, device_id_type=MESH
        )
        made.start()
        started.append(made)
        return made

    ring = {}

    def send_ring(stream, bufs, d):
        up, down = (at(0, 1, 0), b), (at(0, ZN - 1, 0), b)
        src_up, dst_up = bufs[(1 - d) % ZN], bufs[-d % ZN]
        src_down, dst_down = bufs[d - 1], bufs[d]
        if d == ZN // 2:
            low = (slice(None),) * (len(dst_up.shape) - 4) + (pl.ds(0, 4),)
            high = (slice(None),) * (len(dst_up.shape) - 4) + (pl.ds(4, 4),)
            if len(dst_up.shape) == 3:
                low, high = pl.ds(0, 4), pl.ds(4, 4)
            else:
                low, high = (slice(None), pl.ds(0, 4)), (slice(None), pl.ds(4, 4))
            src_up, dst_up = src_up.at[low], dst_up.at[low]
            src_down, dst_down = src_down.at[high], dst_down.at[high]
        ring[stream, d] = (copy(src_up, dst_up, up), copy(src_down, dst_down, down))

    def take_ring(stream, bufs, d):
        for made in ring[stream, d]:
            made.wait_recv()
        if d < ZN // 2:
            send_ring(stream, bufs, d + 1)

    def block_at(e, dx, dy):
        return at(dx, e, dy)

    def pick(which, k, j):
        return table[which * (wedges * MAXB) + k * MAXB + j]

    y_copies, x_copies = {}, {}

    def share(e):
        for dx, bufs in ((0, own0), (1, pair0)):
            k = block_at(e, dx, 0)
            for dy in range(1, YN):
                for j in range(MAXB):
                    y_send[e][dy - 1, dx, j] = bufs[e][pick(dy, k, j)]
        y_copies[e] = [
            copy(y_send[e].at[dy - 1], y_got[e].at[YN - dy - 1], (at(0, 0, dy), b)) for dy in range(1, YN)
        ]
        for dy in range(YN):
            k = block_at(e, 0, dy)
            for j in range(MAXB):
                t = pick(4, k, j)
                x_send[e][dy, j] = own1[e][t] if dy == 0 else column1[e][dy - 1, t]
        x_copies[e] = [copy(x_send[e], x_got[e], (at(1, 0, 0), b))]

    def place(row, k, load):
        tiles = [load(j).astype(jnp.float32) for j in range(MAXB)]
        names = [pick(5, k, j) for j in range(MAXB)]
        row = pl.multiple_of(row, 16)
        for m in range(8):
            total = jnp.zeros((16, TILE), jnp.float32)
            for j in range(MAXB):
                total = total + jnp.where(names[j] == m, tiles[j], 0.0)
            lhs[pl.ds(row, 16), m * TILE : (m + 1) * TILE] = total.astype(jnp.bfloat16)

    def process(es):
        for index, e in enumerate(es):
            for made in y_copies[e] + x_copies[e]:
                made.wait_recv()

            def row_of(q, dx, dy, index=index):
                return index * 256 + q * 128 + lax.rem(x + dx, XN) * 64 + lax.rem(y + dy, YN) * 16

            for dx, bufs in ((0, own0), (1, pair0)):
                k = block_at(e, dx, 0)
                place(row_of(0, dx, 0), k, lambda j: bufs[e][pick(0, k, j)])
            k = block_at(e, 0, 0)
            place(row_of(1, 0, 0), k, lambda j: own1[e][pick(0, k, j)])

            @pl.loop(1, YN)
            def _(dy, e=e, row_of=row_of):
                for dx in range(XN):
                    k = block_at(e, dx, dy)
                    place(row_of(0, dx, dy), k, lambda j: y_got[e][dy - 1, dx, j])
                k = block_at(e, 0, dy)
                place(row_of(1, 0, dy), k, lambda j: column1[e][dy - 1, pick(0, k, j)])

            @pl.loop(0, YN)
            def _(dy, e=e, row_of=row_of):
                k = block_at(e, 1, dy)
                place(row_of(1, 1, dy), k, lambda j: x_got[e][dy, j])

        @pl.loop(0, 4)
        def _(n):
            columns = pl.ds(pl.multiple_of(n * 256, 256), 256)
            rows = 256 * len(es)
            got = jnp.dot(lhs[0:rows, :], bank_v[:, columns], preferred_element_type=jnp.float32)
            got = got.astype(jnp.bfloat16)
            for index, e in enumerate(es):
                for q in range(2):
                    for xa in range(XN):
                        start = q * 1024 + xa * 512 + lax.rem(z + e, ZN) * 64
                        here = index * 256 + q * 128 + xa * 64
                        resampled[pl.ds(pl.multiple_of(start, 64), 64), columns] = got[here : here + 64]

    def slices(d):
        return [0] if d == 0 else [4] if d == 4 else [d, ZN - d]

    first_x = copy(own0[0], pair0[0], (at(1, 0, 0), b))
    send_ring("own0", own0, 1)
    first_y = [copy(own1[0], column1[0].at[YN - dy - 1], (at(0, 0, dy), b)) for dy in range(1, YN)]
    send_ring("own1", own1, 1)
    for turn in range(1, 6):
        if turn <= 4:
            take_ring("own0", own0, turn)
            take_ring("own1", own1, turn)
        if turn == 1:
            first_x.wait_recv()
            send_ring("pair0", pair0, 1)
            for made in first_y:
                made.wait_recv()
            send_ring("column1", column1, 1)
        else:
            take_ring("pair0", pair0, turn - 1)
            take_ring("column1", column1, turn - 1)
        for e in slices(turn - 1):
            share(e)
        if turn == 3:
            for load in loads:
                load.wait()
        if turn >= 3:
            process(slices(turn - 3))
    process(slices(3))
    process(slices(4))

    steer = steer_v[...]
    for n in range(4):
        columns = slice(n * 256, (n + 1) * 256)
        by_real = jnp.dot(steer, resampled[0:1024, columns], preferred_element_type=jnp.float32)
        by_imag = jnp.dot(steer, resampled[1024:2048, columns], preferred_element_type=jnp.float32)
        image[0, :, columns] = by_real[:64] - by_imag[64:]
        image[1, :, columns] = by_imag[:64] + by_real[64:]
    stores = [pltpu.make_async_copy(image, focused_out, load_sem.at[2])]
    stores[0].start()

    rows_send[0] = image[:, 0, :]
    rows_send[1] = image[:, 63, :]
    eye = lax.broadcasted_iota(jnp.int32, (128, 128), 0) == lax.broadcasted_iota(jnp.int32, (128, 128), 1)
    for side, column in ((0, 0), (1, 1023)):
        values = jnp.concatenate([image[0, :, column : column + 1], image[1, :, column : column + 1]], axis=0)
        cols_send[side] = jnp.sum(jnp.where(eye, values, 0.0), axis=0, keepdims=True)
    edge = [
        copy(rows_send.at[0], rows_got.at[1], (before, b)),
        copy(rows_send.at[1], rows_got.at[0], (after, b)),
        copy(cols_send.at[0], cols_got.at[1], (w, lax.rem(b + BN - 1, BN))),
        copy(cols_send.at[1], cols_got.at[0], (w, lax.rem(b + 1, BN))),
    ]

    squared = image[0] * image[0] + image[1] * image[1]
    cubed = jnp.concatenate([squared * image[0], squared * image[1]], axis=0).astype(jnp.bfloat16)
    across = (((1,), (1,)), ((), ()))
    for n in range(8):
        pulses_here = slice(n * 128, (n + 1) * 128)
        late = slice(1024 + n * 128, 1024 + (n + 1) * 128)
        by0 = lax.dot_general(cubed, resampled[pulses_here, :], across, preferred_element_type=jnp.float32)
        by1 = lax.dot_general(cubed, resampled[late, :], across, preferred_element_type=jnp.float32)
        s0 = steer_v[0:64, pulses_here].astype(jnp.float32)
        s1 = steer_v[64:128, pulses_here].astype(jnp.float32)
        terms = s0 * (by1[:64] - by0[64:]) + s1 * (by1[64:] + by0[:64])
        part_one[n] = jnp.sum(terms, axis=0, keepdims=True)
    one = [copy(part_one, got_one.at[ZN - dz - 1], (at(0, dz, 0), b)) for dz in range(1, ZN)]

    for made in edge:
        made.wait_recv()
    row = lax.broadcasted_iota(jnp.int32, (64, 1024), 0)
    col = lax.broadcasted_iota(jnp.int32, (64, 1024), 1)

    def pull(d0, d1):
        inverse = lax.rsqrt(d0 * d0 + d1 * d1 + EDGE_SOFTNESS)
        return d0 * inverse, d1 * inverse

    f = [image[0], image[1]]
    above = [jnp.where(row == 0, rows_got[0, i : i + 1], pltpu.roll(f[i], 1, 0)) for i in range(2)]
    up = pull(f[0] - above[0], f[1] - above[1])
    below = [jnp.where(row == 63, rows_got[1, i : i + 1], pltpu.roll(f[i], 63, 0)) for i in range(2)]
    down = pull(f[0] - below[0], f[1] - below[1])
    beside = []
    for side in range(2):
        values = jnp.sum(jnp.where(eye, cols_got[side], 0.0), axis=1, keepdims=True)
        beside.append([values[:64], values[64:]])
    left = [jnp.where(col == 0, beside[0][i], pltpu.roll(f[i], 1, 1)) for i in range(2)]
    inward = pull(f[0] - left[0], f[1] - left[1])
    right = [jnp.where(col == 1023, beside[1][i], pltpu.roll(f[i], 1023, 1)) for i in range(2)]
    outward = pull(f[0] - right[0], f[1] - right[1])
    lower = (col > 0) | (b > 0)
    upper = (col < 1023) | (b < BN - 1)
    for i in range(2):
        total = up[i] + down[i] + jnp.where(lower, inward[i], 0.0) + jnp.where(upper, outward[i], 0.0)
        smooth[i] = f[i] - STEP_SIZE * total
    stores.append(pltpu.make_async_copy(smooth, smoothed_out, load_sem.at[3]))
    stores[1].start()

    for made in one:
        made.wait_recv()
    total = part_one[...]
    for i in range(ZN - 1):
        total = total + got_one[i]
    part_two[...] = total
    two = []
    for i, (dx, dy, db) in enumerate(plane):
        other = plane.index(((XN - dx) % XN, (YN - dy) % YN, (BN - db) % BN))
        source = part_two.at[lax.rem(x + dx, XN) * 4 + z // 2]
        two.append(copy(source, got_two.at[other], (at(dx, 0, dy), lax.rem(b + db, BN))))
    for made in two:
        made.wait_recv()
    row_sum = part_two[x * 4 + z // 2]
    for i in range(len(plane)):
        row_sum = row_sum + got_two[i]
    offset = lax.rem(z, 2) * 64 + y * 16
    gradient_out[...] = pltpu.roll(jnp.broadcast_to(row_sum, (8, TILE)), lax.rem(TILE - offset, TILE), 1)[0:1, :16] * scale

    for made in started:
        made.wait_send()
    for store in stores:
        store.wait()


def shards(pulse_data, phase_error, steering, kernel_bank, tile_offsets, kernel_ids, counts):
    w = lax.axis_index("wedge")
    x, z, y = w // (ZN * YN), (w // YN) % ZN, w % YN
    near = [w] + [x * 32 + z * 4 + (y + dy) % YN for dy in range(1, YN)] + [(w + 32) % 64]
    rows = [lax.dynamic_index_in_dim(tile_offsets, k, 1, keepdims=False) for k in near]
    ids = lax.dynamic_index_in_dim(kernel_ids, w, 1, keepdims=False)
    live = lax.dynamic_index_in_dim(counts, w, 1, keepdims=False)
    ids = jnp.where(jnp.arange(MAXB)[None, :] < live[:, None], ids, 8)
    table = jnp.reshape(jnp.stack(rows + [ids]), (-1,))
    bf, f32 = jnp.bfloat16, jnp.float32
    block = pltpu.VMEM((8, 16, TILE), bf)
    scratch = [block] * 24
    scratch += [pltpu.VMEM((3, 8, 16, TILE), bf)] * 8
    scratch += [pltpu.VMEM((3, 2, 4, 16, TILE), bf)] * 16
    scratch += [pltpu.VMEM((4, 4, 16, TILE), bf)] * 16
    scratch += [
        pltpu.VMEM((512, 1024), bf),
        pltpu.VMEM((2048, 1024), bf),
        pltpu.VMEM((1024, 1024), bf),
        pltpu.VMEM((128, 1024), bf),
        pltpu.VMEM((2, 64, 1024), f32),
        pltpu.VMEM((2, 64, 1024), f32),
        pltpu.VMEM((2, 2, 1024), f32),
        pltpu.VMEM((2, 2, 1024), f32),
        pltpu.VMEM((2, 1, TILE), f32),
        pltpu.VMEM((2, 1, TILE), f32),
        pltpu.VMEM((8, 1, TILE), f32),
        pltpu.VMEM((7, 8, 1, TILE), f32),
        pltpu.VMEM((8, 1, TILE), f32),
        pltpu.VMEM((31, 1, TILE), f32),
        pltpu.SemaphoreType.DMA((COPIES,)),
        pltpu.SemaphoreType.DMA((COPIES,)),
        pltpu.SemaphoreType.DMA((4,)),
    ]
    scale = math.sqrt(1024 / (4096 * 4096))
    image = jax.ShapeDtypeStruct((2, 64, 1024), f32)
    vmem = pl.BlockSpec(memory_space=pltpu.VMEM)
    anywhere = pl.BlockSpec(memory_space=pl.ANY)
    focused, smoothed, gradient = pl.pallas_call(
        functools.partial(kernel, scale),
        out_shape=(image, image, jax.ShapeDtypeStruct((1, 16), f32)),
        in_specs=[pl.BlockSpec(memory_space=pltpu.SMEM), vmem, vmem, anywhere, anywhere],
        out_specs=(anywhere, anywhere, vmem),
        scratch_shapes=scratch,
        compiler_params=pltpu.CompilerParams(
            collective_id=0, has_side_effects=True, vmem_limit_bytes=40 << 20
        ),
    )(
        table,
        jnp.reshape(phase_error, (1, 16)),
        pulse_data,
        jnp.reshape(steering, (128, 1024)),
        jnp.reshape(kernel_bank, (1024, 1024)),
    )
    return focused, smoothed, jnp.reshape(gradient, (16,))


def solution(mesh):
    in_specs = (
        P(None, "wedge", "band"),
        P("wedge"),
        P(None, "wedge", None),
        P(None, None, "band"),
        P(),
        P(),
        P(),
    )
    out_specs = (P(None, "wedge", "band"), P(None, "wedge", "band"), P("wedge"))
    return jax.shard_map(shards, mesh=mesh, in_specs=in_specs, out_specs=out_specs, check_vma=False)
```

```python
import functools
import math

import jax
import jax.numpy as jnp
from jax import lax
from jax.experimental import pallas as pl
from jax.experimental.pallas import tpu as pltpu
from jax.sharding import PartitionSpec as P

TILE = 128
MAXB = 4
EDGE_SOFTNESS = 0.05
STEP_SIZE = 0.25
XN, ZN, YN, BN = 2, 8, 4, 4
MESH = pl.DeviceIdType.MESH
COPIES = 192


def kernel(scale, offsets_in, ids_in, counts_in, phase_in, pulses_in, steering, bank, focused_out, smoothed_out, gradient_out, *scratch):
    scratch = list(scratch)
    take = lambda n: [scratch.pop(0) for _ in range(n)]
    own0, pair0, own1 = take(ZN), take(ZN), take(ZN)
    column1 = take(ZN)
    y_send, y_got = take(ZN), take(ZN)
    x_send, x_got = take(ZN), take(ZN)
    lhs, resampled, bank_v, steer_v, image, smooth = take(6)
    rows_send, rows_got, cols_send, cols_got = take(4)
    part_one, got_one, part_two, got_two = take(4)
    offsets, ids, counts, phase, pulses, table_v, table = take(7)
    send_sem, recv_sem, load_sem = take(3)

    w = lax.axis_index("wedge")
    b = lax.axis_index("band")
    x, z, y = w // (ZN * YN), lax.rem(w // YN, ZN), lax.rem(w, YN)

    def at(dx, dz, dy):
        return lax.rem(x + dx, XN) * (ZN * YN) + lax.rem(z + dz, ZN) * YN + lax.rem(y + dy, YN)

    def load(src, dst, n):
        made = pltpu.make_async_copy(src, dst, load_sem.at[n])
        made.start()
        return made

    first_loads = [load(pulses_in, pulses, 4), load(phase_in, phase, 5)]
    index_loads = [load(offsets_in, offsets, 6), load(ids_in, ids, 7), load(counts_in, counts, 8)]
    loads = [load(bank, bank_v, 0), load(steering, steer_v, 1)]

    wedges = XN * ZN * YN
    after, before = lax.rem(w + 1, wedges), lax.rem(w + wedges - 1, wedges)
    greeted = [(at(0, 1, 0), b), (at(0, ZN - 1, 0), b), (at(1, 0, 0), b)]
    greeted += [(at(0, 0, dy), b) for dy in range(1, YN)]
    greeted += [(w, lax.rem(b + db, BN)) for db in range(1, BN)]
    barrier = pltpu.get_barrier_semaphore()
    for device in greeted:
        pl.semaphore_signal(barrier, inc=1, device_id=device, device_id_type=MESH)

    square = lax.broadcasted_iota(jnp.int32, (16, 16), 0) == lax.broadcasted_iota(jnp.int32, (16, 16), 1)
    for made in first_loads:
        made.wait()
    angle = jnp.sum(jnp.where(square, phase[...], 0.0), axis=1, keepdims=True)
    cosine, sine = jnp.cos(angle), jnp.sin(angle)
    real, imag = pulses[0].astype(jnp.float32), pulses[1].astype(jnp.float32)
    fixed0 = (real * cosine + imag * sine).astype(jnp.bfloat16)
    fixed1 = (imag * cosine - real * sine).astype(jnp.bfloat16)
    for t in range(8):
        own0[0][t] = fixed0[:, t * TILE : (t + 1) * TILE]
        own1[0][t] = fixed1[:, t * TILE : (t + 1) * TILE]

    pl.semaphore_wait(barrier, len(greeted))

    started = []

    def copy(src, dst, device):
        index = len(started)
        made = pltpu.make_async_remote_copy(
            src, dst, send_sem.at[index], recv_sem.at[index], device_id=device, device_id_type=MESH
        )
        made.start()
        started.append(made)
        return made

    ring = {}

    def send_ring(stream, bufs, d):
        up, down = (at(0, 1, 0), b), (at(0, ZN - 1, 0), b)
        src_up, dst_up = bufs[(1 - d) % ZN], bufs[-d % ZN]
        src_down, dst_down = bufs[d - 1], bufs[d]
        if d == ZN // 2:
            low = (slice(None),) * (len(dst_up.shape) - 4) + (pl.ds(0, 4),)
            high = (slice(None),) * (len(dst_up.shape) - 4) + (pl.ds(4, 4),)
            if len(dst_up.shape) == 3:
                low, high = pl.ds(0, 4), pl.ds(4, 4)
            else:
                low, high = (slice(None), pl.ds(0, 4)), (slice(None), pl.ds(4, 4))
            src_up, dst_up = src_up.at[low], dst_up.at[low]
            src_down, dst_down = src_down.at[high], dst_down.at[high]
        ring[stream, d] = (copy(src_up, dst_up, up), copy(src_down, dst_down, down))

    def take_ring(stream, bufs, d):
        for made in ring[stream, d]:
            made.wait_recv()
        if d < ZN // 2:
            send_ring(stream, bufs, d + 1)

    def block_at(e, dx, dy):
        return at(dx, e, dy)

    def pick(which, k, j):
        return table[which, k * MAXB + j]

    y_copies, x_copies = {}, {}

    def share(e):
        for dx, bufs in ((0, own0), (1, pair0)):
            k = block_at(e, dx, 0)
            for dy in range(1, YN):
                for j in range(MAXB):
                    y_send[e][dy - 1, dx, j] = bufs[e][pick(dy, k, j)]
        y_copies[e] = [
            copy(y_send[e].at[dy - 1], y_got[e].at[YN - dy - 1], (at(0, 0, dy), b)) for dy in range(1, YN)
        ]
        for dy in range(YN):
            k = block_at(e, 0, dy)
            for j in range(MAXB):
                t = pick(4, k, j)
                x_send[e][dy, j] = own1[e][t] if dy == 0 else column1[e][dy - 1, t]
        x_copies[e] = [copy(x_send[e], x_got[e], (at(1, 0, 0), b))]

    def place(row, k, load):
        tiles = [load(j).astype(jnp.float32) for j in range(MAXB)]
        names = [jnp.where(j < table[6, k], pick(5, k, j), 8) for j in range(MAXB)]
        row = pl.multiple_of(row, 16)
        for m in range(8):
            total = jnp.zeros((16, TILE), jnp.float32)
            for j in range(MAXB):
                total = total + jnp.where(names[j] == m, tiles[j], 0.0)
            lhs[pl.ds(row, 16), m * TILE : (m + 1) * TILE] = total.astype(jnp.bfloat16)

    def process(es):
        for index, e in enumerate(es):
            for made in y_copies[e] + x_copies[e]:
                made.wait_recv()

            def row_of(q, dx, dy, index=index):
                return index * 256 + q * 128 + lax.rem(x + dx, XN) * 64 + lax.rem(y + dy, YN) * 16

            for dx, bufs in ((0, own0), (1, pair0)):
                k = block_at(e, dx, 0)
                place(row_of(0, dx, 0), k, lambda j: bufs[e][pick(0, k, j)])
            k = block_at(e, 0, 0)
            place(row_of(1, 0, 0), k, lambda j: own1[e][pick(0, k, j)])

            @pl.loop(1, YN)
            def _(dy, e=e, row_of=row_of):
                for dx in range(XN):
                    k = block_at(e, dx, dy)
                    place(row_of(0, dx, dy), k, lambda j: y_got[e][dy - 1, dx, j])
                k = block_at(e, 0, dy)
                place(row_of(1, 0, dy), k, lambda j: column1[e][dy - 1, pick(0, k, j)])

            @pl.loop(0, YN)
            def _(dy, e=e, row_of=row_of):
                k = block_at(e, 1, dy)
                place(row_of(1, 1, dy), k, lambda j: x_got[e][dy, j])

        @pl.loop(0, 4)
        def _(n):
            columns = pl.ds(pl.multiple_of(n * 256, 256), 256)
            rows = 256 * len(es)
            got = jnp.dot(lhs[0:rows, :], bank_v[:, columns], preferred_element_type=jnp.float32)
            got = got.astype(jnp.bfloat16)
            for index, e in enumerate(es):
                for q in range(2):
                    for xa in range(XN):
                        start = q * 1024 + xa * 512 + lax.rem(z + e, ZN) * 64
                        here = index * 256 + q * 128 + xa * 64
                        resampled[pl.ds(pl.multiple_of(start, 64), 64), columns] = got[here : here + 64]

    def slices(d):
        return [0] if d == 0 else [4] if d == 4 else [d, ZN - d]

    first_x = copy(own0[0], pair0[0], (at(1, 0, 0), b))
    send_ring("own0", own0, 1)
    first_y = [copy(own1[0], column1[0].at[YN - dy - 1], (at(0, 0, dy), b)) for dy in range(1, YN)]
    send_ring("own1", own1, 1)

    for made in index_loads:
        made.wait()
    near = [w] + [at(0, 0, dy) for dy in range(1, YN)] + [at(1, 0, 0), w, w]
    kind = lax.broadcasted_iota(jnp.int32, (8, wedges), 0)
    lane = lax.broadcasted_iota(jnp.int32, (8, wedges), 1)
    wanted = jnp.zeros((8, wedges), jnp.int32)
    for n, wedge in enumerate(near):
        wanted = jnp.where(kind == n, wedge, wanted)
    chosen = jnp.where(lane == wanted, 1.0, 0.0).astype(jnp.bfloat16)
    across = (((1,), (1,)), ((), ()))

    def choose(ref, rows):
        values = jnp.reshape(ref[...], (rows, wedges)).astype(jnp.float32).astype(jnp.bfloat16)
        return lax.dot_general(chosen, values, across, preferred_element_type=jnp.float32).astype(jnp.int32)

    row = lax.broadcasted_iota(jnp.int32, (8, wedges * MAXB), 0)
    picked = jnp.where(row == 5, choose(ids, wedges * MAXB), choose(offsets, wedges * MAXB))
    table_v[...] = jnp.clip(picked, 0, 7)
    table_v[6:7, 0:wedges] = choose(counts, wedges)[6:7]
    load(table_v, table, 9).wait()
    for turn in range(1, 6):
        if turn <= 4:
            take_ring("own0", own0, turn)
            take_ring("own1", own1, turn)
        if turn == 1:
            first_x.wait_recv()
            send_ring("pair0", pair0, 1)
            for made in first_y:
                made.wait_recv()
            send_ring("column1", column1, 1)
        else:
            take_ring("pair0", pair0, turn - 1)
            take_ring("column1", column1, turn - 1)
        for e in slices(turn - 1):
            share(e)
        if turn == 2:
            for made in loads:
                made.wait()
        if turn >= 2:
            process(slices(turn - 2))
    process(slices(4))

    steer = steer_v[...]
    for n in range(4):
        columns = slice(n * 256, (n + 1) * 256)
        by_real = jnp.dot(steer, resampled[0:1024, columns], preferred_element_type=jnp.float32)
        by_imag = jnp.dot(steer, resampled[1024:2048, columns], preferred_element_type=jnp.float32)
        image[0, :, columns] = by_real[:64] - by_imag[64:]
        image[1, :, columns] = by_imag[:64] + by_real[64:]
    stores = [pltpu.make_async_copy(image, focused_out, load_sem.at[2])]
    stores[0].start()

    rows_send[0] = image[:, 0, :]
    rows_send[1] = image[:, 63, :]
    eye = lax.broadcasted_iota(jnp.int32, (128, 128), 0) == lax.broadcasted_iota(jnp.int32, (128, 128), 1)
    for side, column in ((0, 0), (1, 1023)):
        values = jnp.concatenate([image[0, :, column : column + 1], image[1, :, column : column + 1]], axis=0)
        cols_send[side] = jnp.sum(jnp.where(eye, values, 0.0), axis=0, keepdims=True)
    edge = [
        copy(rows_send.at[0], rows_got.at[1], (before, b)),
        copy(rows_send.at[1], rows_got.at[0], (after, b)),
        copy(cols_send.at[0], cols_got.at[1], (w, lax.rem(b + BN - 1, BN))),
        copy(cols_send.at[1], cols_got.at[0], (w, lax.rem(b + 1, BN))),
    ]

    squared = image[0] * image[0] + image[1] * image[1]
    cubed = jnp.concatenate([squared * image[0], squared * image[1]], axis=0).astype(jnp.bfloat16)
    for n in range(8):
        pulses_here = slice(n * 128, (n + 1) * 128)
        late = slice(1024 + n * 128, 1024 + (n + 1) * 128)
        by0 = lax.dot_general(cubed, resampled[pulses_here, :], across, preferred_element_type=jnp.float32)
        by1 = lax.dot_general(cubed, resampled[late, :], across, preferred_element_type=jnp.float32)
        s0 = steer_v[0:64, pulses_here].astype(jnp.float32)
        s1 = steer_v[64:128, pulses_here].astype(jnp.float32)
        terms = s0 * (by1[:64] - by0[64:]) + s1 * (by1[64:] + by0[:64])
        part_one[n] = jnp.sum(terms, axis=0, keepdims=True)
    core, half = lax.rem(b, 2), b // 2
    first_group = [(dz, dc) for dc in range(2) for dz in range(ZN) if (dz, dc) != (0, 0)]
    one = []
    for dz, dc in first_group:
        other = first_group.index(((ZN - dz) % ZN, dc))
        one.append(copy(part_one, got_one.at[other], (at(0, dz, 0), half * 2 + lax.rem(core + dc, 2))))

    for made in edge:
        made.wait_recv()
    row = lax.broadcasted_iota(jnp.int32, (64, 1024), 0)
    col = lax.broadcasted_iota(jnp.int32, (64, 1024), 1)

    def pull(d0, d1):
        inverse = lax.rsqrt(d0 * d0 + d1 * d1 + EDGE_SOFTNESS)
        return d0 * inverse, d1 * inverse

    f = [image[0], image[1]]
    above = [jnp.where(row == 0, rows_got[0, i : i + 1], pltpu.roll(f[i], 1, 0)) for i in range(2)]
    up = pull(f[0] - above[0], f[1] - above[1])
    below = [jnp.where(row == 63, rows_got[1, i : i + 1], pltpu.roll(f[i], 63, 0)) for i in range(2)]
    down = pull(f[0] - below[0], f[1] - below[1])
    beside = []
    for side in range(2):
        values = jnp.sum(jnp.where(eye, cols_got[side], 0.0), axis=1, keepdims=True)
        beside.append([values[:64], values[64:]])
    left = [jnp.where(col == 0, beside[0][i], pltpu.roll(f[i], 1, 1)) for i in range(2)]
    inward = pull(f[0] - left[0], f[1] - left[1])
    right = [jnp.where(col == 1023, beside[1][i], pltpu.roll(f[i], 1023, 1)) for i in range(2)]
    outward = pull(f[0] - right[0], f[1] - right[1])
    lower = (col > 0) | (b > 0)
    upper = (col < 1023) | (b < BN - 1)
    for i in range(2):
        total = up[i] + down[i] + jnp.where(lower, inward[i], 0.0) + jnp.where(upper, outward[i], 0.0)
        smooth[i] = f[i] - STEP_SIZE * total
    stores.append(pltpu.make_async_copy(smooth, smoothed_out, load_sem.at[3]))
    stores[1].start()

    for made in one:
        made.wait_recv()
    total = part_one[...]
    for i in range(len(first_group)):
        total = total + got_one[i]
    part_two[...] = total
    second_group = [(dh, dx, dy) for dh in range(2) for dx in range(XN) for dy in range(YN) if (dh, dx, dy) != (0, 0, 0)]
    two = []
    for dh, dx, dy in second_group:
        other = second_group.index((dh, dx, (YN - dy) % YN))
        source = part_two.at[lax.rem(x + dx, XN) * 4 + z // 2]
        two.append(copy(source, got_two.at[other], (at(dx, 0, dy), lax.rem(half + dh, 2) * 2 + core)))
    for made in two:
        made.wait_recv()
    row_sum = part_two[x * 4 + z // 2]
    for i in range(len(second_group)):
        row_sum = row_sum + got_two[i]
    offset = lax.rem(z, 2) * 64 + y * 16
    turned = pltpu.roll(jnp.broadcast_to(row_sum, (8, TILE)), lax.rem(TILE - offset, TILE), 1)
    gradient_out[...] = turned[0:1, :16] * scale

    for made in started:
        made.wait_send()
    for store in stores:
        store.wait()


def hand_on(focused, smoothed, gradient, focused_out, smoothed_out, gradient_out, held, row, sem):
    moves = [
        (src.at[q, pl.ds(h * 32, 32)], held.at[n, q, pl.ds(h * 32, 32)], dst.at[q, pl.ds(h * 32, 32)])
        for n, (src, dst) in enumerate(((focused, focused_out), (smoothed, smoothed_out)))
        for q in range(2)
        for h in range(2)
    ]
    moves.append((gradient, row, gradient_out))
    loads = [pltpu.make_async_copy(src, mid, sem.at[0, n]) for n, (src, mid, _) in enumerate(moves)]
    stores = [pltpu.make_async_copy(mid, dst, sem.at[1, n]) for n, (_, mid, dst) in enumerate(moves)]
    for made in loads:
        made.start()
    for made, store in zip(loads, stores):
        made.wait()
        store.start()
    for made in stores:
        made.wait()


def shards(pulse_data, phase_error, steering, kernel_bank, tile_offsets, kernel_ids, counts):
    bf, f32 = jnp.bfloat16, jnp.float32
    block = pltpu.VMEM((8, 16, TILE), bf)
    scratch = [block] * 24
    scratch += [pltpu.VMEM((3, 8, 16, TILE), bf)] * 8
    scratch += [pltpu.VMEM((3, 2, 4, 16, TILE), bf)] * 16
    scratch += [pltpu.VMEM((4, 4, 16, TILE), bf)] * 16
    scratch += [
        pltpu.VMEM((512, 1024), bf),
        pltpu.VMEM((2048, 1024), bf),
        pltpu.VMEM((1024, 1024), bf),
        pltpu.VMEM((128, 1024), bf),
        pltpu.VMEM((2, 64, 1024), f32),
        pltpu.VMEM((2, 64, 1024), f32),
        pltpu.VMEM((2, 2, 1024), f32),
        pltpu.VMEM((2, 2, 1024), f32),
        pltpu.VMEM((2, 1, TILE), f32),
        pltpu.VMEM((2, 1, TILE), f32),
        pltpu.VMEM((8, 1, TILE), f32),
        pltpu.VMEM((15, 8, 1, TILE), f32),
        pltpu.VMEM((8, 1, TILE), f32),
        pltpu.VMEM((15, 1, TILE), f32),
        pltpu.VMEM((64, MAXB, 64), jnp.int32),
        pltpu.VMEM((64, MAXB, 64), jnp.int32),
        pltpu.VMEM((64, 64), jnp.int32),
        pltpu.VMEM((1, 16), f32),
        pltpu.VMEM((2, 16, 1024), bf),
        pltpu.VMEM((8, 256), jnp.int32),
        pltpu.SMEM((8, 256), jnp.int32),
        pltpu.SemaphoreType.DMA((COPIES,)),
        pltpu.SemaphoreType.DMA((COPIES,)),
        pltpu.SemaphoreType.DMA((10,)),
    ]
    scale = math.sqrt(1024 / (4096 * 4096))
    image = jax.ShapeDtypeStruct((2, 64, 1024), f32)
    vmem = pl.BlockSpec(memory_space=pltpu.VMEM)
    anywhere = pl.BlockSpec(memory_space=pl.ANY)
    focused, smoothed, gradient = pl.pallas_call(
        functools.partial(kernel, scale),
        out_shape=(image, image, jax.ShapeDtypeStruct((1, 16), f32)),
        in_specs=[anywhere] * 7,
        out_specs=(anywhere, anywhere, vmem),
        scratch_shapes=scratch,
        compiler_params=pltpu.CompilerParams(
            collective_id=0, has_side_effects=True, vmem_limit_bytes=62 << 20
        ),
    )(
        jnp.transpose(tile_offsets, (0, 2, 1)),
        jnp.transpose(kernel_ids, (0, 2, 1)),
        counts,
        jnp.reshape(phase_error, (1, 16)),
        pulse_data,
        jnp.reshape(steering, (128, 1024)),
        jnp.reshape(kernel_bank, (1024, 1024)),
    )
    results = pl.pallas_call(
        hand_on,
        out_shape=(image, image, jax.ShapeDtypeStruct((1, 16), f32)),
        in_specs=[anywhere] * 3,
        out_specs=[anywhere] * 3,
        scratch_shapes=[pltpu.VMEM((2, 2, 64, 1024), f32), pltpu.VMEM((1, 16), f32), pltpu.SemaphoreType.DMA((2, 9))],
        compiler_params=pltpu.CompilerParams(vmem_limit_bytes=62 << 20),
    )(focused, smoothed, gradient)
    return results[0], results[1], jnp.reshape(results[2], (16,))


def solution(mesh):
    in_specs = (
        P(None, "wedge", "band"),
        P("wedge"),
        P(None, "wedge", None),
        P(None, None, "band"),
        P(),
        P(),
        P(),
    )
    out_specs = (P(None, "wedge", "band"), P(None, "wedge", "band"), P("wedge"))
    return jax.shard_map(shards, mesh=mesh, in_specs=in_specs, out_specs=out_specs, check_vma=False)
```

```python
import functools
import math

import jax
import jax.numpy as jnp
from jax import lax
from jax.experimental import pallas as pl
from jax.experimental.pallas import tpu as pltpu
from jax.sharding import PartitionSpec as P

TILE = 128
MAXB = 4
EDGE_SOFTNESS = 0.05
STEP_SIZE = 0.25
XN, ZN, YN, BN = 2, 8, 4, 4
MESH = pl.DeviceIdType.MESH
COPIES = 192


def kernel(scale, offsets_in, ids_in, counts_in, phase_in, pulses_in, steering, bank, focused_out, smoothed_out, gradient_out, *scratch):
    scratch = list(scratch)
    take = lambda n: [scratch.pop(0) for _ in range(n)]
    own0, pair0, own1 = take(ZN), take(ZN), take(ZN)
    column1 = take(ZN)
    y_send, y_got = take(ZN), take(ZN)
    x_send, x_got = take(ZN), take(ZN)
    lhs, resampled, bank_v, steer_v, image, smooth = take(6)
    rows_send, rows_got, cols_send, cols_got = take(4)
    part_one, got_one, part_two, got_two = take(4)
    offsets, ids, counts, phase, pulses, table_v, table = take(7)
    send_sem, recv_sem, load_sem = take(3)

    w = lax.axis_index("wedge")
    b = lax.axis_index("band")
    x, z, y = w // (ZN * YN), lax.rem(w // YN, ZN), lax.rem(w, YN)

    def at(dx, dz, dy):
        return lax.rem(x + dx, XN) * (ZN * YN) + lax.rem(z + dz, ZN) * YN + lax.rem(y + dy, YN)

    def load(src, dst, n):
        made = pltpu.make_async_copy(src, dst, load_sem.at[n])
        made.start()
        return made

    first_loads = [load(pulses_in, pulses, 4), load(phase_in, phase, 5)]
    index_loads = [load(offsets_in, offsets, 6), load(ids_in, ids, 7), load(counts_in, counts, 8)]
    loads = [load(bank, bank_v, 0), load(steering, steer_v, 1)]

    wedges = XN * ZN * YN
    after, before = lax.rem(w + 1, wedges), lax.rem(w + wedges - 1, wedges)
    greeted = [(at(0, 1, 0), b), (at(0, ZN - 1, 0), b), (at(1, 0, 0), b)]
    greeted += [(at(0, 0, dy), b) for dy in range(1, YN)]
    greeted += [(w, lax.rem(b + db, BN)) for db in range(1, BN)]
    barrier = pltpu.get_barrier_semaphore()
    for device in greeted:
        pl.semaphore_signal(barrier, inc=1, device_id=device, device_id_type=MESH)

    square = lax.broadcasted_iota(jnp.int32, (16, 16), 0) == lax.broadcasted_iota(jnp.int32, (16, 16), 1)
    for made in first_loads:
        made.wait()
    angle = jnp.sum(jnp.where(square, phase[...], 0.0), axis=1, keepdims=True)
    cosine, sine = jnp.cos(angle), jnp.sin(angle)
    real, imag = pulses[0].astype(jnp.float32), pulses[1].astype(jnp.float32)
    fixed0 = (real * cosine + imag * sine).astype(jnp.bfloat16)
    fixed1 = (imag * cosine - real * sine).astype(jnp.bfloat16)
    for t in range(8):
        own0[0][t] = fixed0[:, t * TILE : (t + 1) * TILE]
        own1[0][t] = fixed1[:, t * TILE : (t + 1) * TILE]

    pl.semaphore_wait(barrier, len(greeted))

    started = []

    def copy(src, dst, device):
        index = len(started)
        made = pltpu.make_async_remote_copy(
            src, dst, send_sem.at[index], recv_sem.at[index], device_id=device, device_id_type=MESH
        )
        made.start()
        started.append(made)
        return made

    ring = {}
    own0_ring = (own0, None)
    own1_ring = (own1, None)
    pair0_ring = (pair0, None)
    column1_rings = [(column1, i) for i in range(YN - 1)]

    def part(ref, index, half):
        if index is None:
            return ref if half is None else ref.at[half]
        return ref.at[index] if half is None else ref.at[index, half]

    def send_ring(name, d, sign):
        bufs, index = name
        key = (id(bufs), index)
        half = None if d < ZN // 2 else pl.ds(0, 4) if sign > 0 else pl.ds(4, 4)
        src = part(bufs[(-sign * (d - 1)) % ZN], index, half)
        dst = part(bufs[(-sign * d) % ZN], index, half)
        ring[key, d, sign] = copy(src, dst, (at(0, sign % ZN, 0), b))

    def start_ring(name):
        for sign in (1, -1):
            send_ring(name, 1, sign)

    def take_ring(name, d):
        for sign in (1, -1):
            ring[(id(name[0]), name[1]), d, sign].wait_recv()
            if d < ZN // 2:
                send_ring(name, d + 1, sign)

    def block_at(e, dx, dy):
        return at(dx, e, dy)

    def pick(which, k, j):
        return table[which, k * MAXB + j]

    y_copies, x_copies = {}, {}

    def share_y(e):
        for dx, bufs in ((0, own0), (1, pair0)):
            k = block_at(e, dx, 0)
            for dy in range(1, YN):
                for j in range(MAXB):
                    y_send[e][dy - 1, dx, j] = bufs[e][pick(dy, k, j)]
        y_copies[e] = [
            copy(y_send[e].at[dy - 1], y_got[e].at[YN - dy - 1], (at(0, 0, dy), b)) for dy in range(1, YN)
        ]

    def share_own(e):
        k = block_at(e, 0, 0)
        for j in range(MAXB):
            x_send[e][0, j] = own1[e][pick(4, k, j)]
        x_copies[e] = [copy(x_send[e].at[0], x_got[e].at[0], (at(1, 0, 0), b))]

    def share_column(e):
        for dy in range(1, YN):
            k = block_at(e, 0, dy)
            for j in range(MAXB):
                x_send[e][dy, j] = column1[e][dy - 1, pick(4, k, j)]
        x_copies[e] += [copy(x_send[e].at[pl.ds(1, 3)], x_got[e].at[pl.ds(1, 3)], (at(1, 0, 0), b))]

    def place(row, k, load):
        tiles = [load(j).astype(jnp.float32) for j in range(MAXB)]
        names = [jnp.where(j < table[6, k], pick(5, k, j), 8) for j in range(MAXB)]
        row = pl.multiple_of(row, 16)
        for m in range(8):
            total = jnp.zeros((16, TILE), jnp.float32)
            for j in range(MAXB):
                total = total + jnp.where(names[j] == m, tiles[j], 0.0)
            lhs[pl.ds(row, 16), m * TILE : (m + 1) * TILE] = total.astype(jnp.bfloat16)

    def process(es):
        for index, e in enumerate(es):
            for made in y_copies[e] + x_copies[e]:
                made.wait_recv()

            def row_of(q, dx, dy, index=index):
                return index * 256 + q * 128 + lax.rem(x + dx, XN) * 64 + lax.rem(y + dy, YN) * 16

            for dx, bufs in ((0, own0), (1, pair0)):
                k = block_at(e, dx, 0)
                place(row_of(0, dx, 0), k, lambda j: bufs[e][pick(0, k, j)])
            k = block_at(e, 0, 0)
            place(row_of(1, 0, 0), k, lambda j: own1[e][pick(0, k, j)])

            @pl.loop(1, YN)
            def _(dy, e=e, row_of=row_of):
                for dx in range(XN):
                    k = block_at(e, dx, dy)
                    place(row_of(0, dx, dy), k, lambda j: y_got[e][dy - 1, dx, j])
                k = block_at(e, 0, dy)
                place(row_of(1, 0, dy), k, lambda j: column1[e][dy - 1, pick(0, k, j)])

            @pl.loop(0, YN)
            def _(dy, e=e, row_of=row_of):
                k = block_at(e, 1, dy)
                place(row_of(1, 1, dy), k, lambda j: x_got[e][dy, j])

        @pl.loop(0, 4)
        def _(n):
            columns = pl.ds(pl.multiple_of(n * 256, 256), 256)
            rows = 256 * len(es)
            got = jnp.dot(lhs[0:rows, :], bank_v[:, columns], preferred_element_type=jnp.float32)
            got = got.astype(jnp.bfloat16)
            for index, e in enumerate(es):
                for q in range(2):
                    for xa in range(XN):
                        start = q * 1024 + xa * 512 + lax.rem(z + e, ZN) * 64
                        here = index * 256 + q * 128 + xa * 64
                        resampled[pl.ds(pl.multiple_of(start, 64), 64), columns] = got[here : here + 64]

    def slices(d):
        return [0] if d == 0 else [4] if d == 4 else [d, ZN - d]

    first_x = copy(own0[0], pair0[0], (at(1, 0, 0), b))
    start_ring(own0_ring)
    first_y = {
        YN - dy - 1: copy(own1[0], column1[0].at[YN - dy - 1], (at(0, 0, dy), b)) for dy in (1, YN - 1)
    }
    start_ring(own1_ring)
    first_y[1] = copy(own1[0], column1[0].at[1], (at(0, 0, 2), b))

    for made in index_loads:
        made.wait()
    near = [w] + [at(0, 0, dy) for dy in range(1, YN)] + [at(1, 0, 0), w, w]
    kind = lax.broadcasted_iota(jnp.int32, (8, wedges), 0)
    lane = lax.broadcasted_iota(jnp.int32, (8, wedges), 1)
    wanted = jnp.zeros((8, wedges), jnp.int32)
    for n, wedge in enumerate(near):
        wanted = jnp.where(kind == n, wedge, wanted)
    chosen = jnp.where(lane == wanted, 1.0, 0.0).astype(jnp.bfloat16)
    across = (((1,), (1,)), ((), ()))

    def choose(ref, rows):
        values = jnp.reshape(ref[...], (rows, wedges)).astype(jnp.float32).astype(jnp.bfloat16)
        return lax.dot_general(chosen, values, across, preferred_element_type=jnp.float32).astype(jnp.int32)

    row = lax.broadcasted_iota(jnp.int32, (8, wedges * MAXB), 0)
    picked = jnp.where(row == 5, choose(ids, wedges * MAXB), choose(offsets, wedges * MAXB))
    table_v[...] = jnp.clip(picked, 0, 7)
    table_v[6:7, 0:wedges] = choose(counts, wedges)[6:7]
    load(table_v, table, 9).wait()
    share_own(0)
    first_x.wait_recv()
    start_ring(pair0_ring)
    take_ring(own0_ring, 1)
    for i in (2, 0):
        first_y[i].wait_recv()
        start_ring(column1_rings[i])
    share_y(0)
    take_ring(own1_ring, 1)
    for e in slices(1):
        share_own(e)
    first_y[1].wait_recv()
    start_ring(column1_rings[1])
    share_column(0)
    for d in range(1, 5):
        take_ring(pair0_ring, d)
        if d < 4:
            take_ring(own0_ring, d + 1)
        for e in slices(d):
            share_y(e)
        for i in (2, 0):
            take_ring(column1_rings[i], d)
        if d < 4:
            take_ring(own1_ring, d + 1)
            for e in slices(d + 1):
                share_own(e)
        take_ring(column1_rings[1], d)
        for e in slices(d):
            share_column(e)
        if d == 1:
            for made in loads:
                made.wait()
        process(slices(d - 1))
    process(slices(4))

    steer = steer_v[...]
    for n in range(4):
        columns = slice(n * 256, (n + 1) * 256)
        by_real = jnp.dot(steer, resampled[0:1024, columns], preferred_element_type=jnp.float32)
        by_imag = jnp.dot(steer, resampled[1024:2048, columns], preferred_element_type=jnp.float32)
        image[0, :, columns] = by_real[:64] - by_imag[64:]
        image[1, :, columns] = by_imag[:64] + by_real[64:]
    stores = [pltpu.make_async_copy(image, focused_out, load_sem.at[2])]
    stores[0].start()

    rows_send[0] = image[:, 0, :]
    rows_send[1] = image[:, 63, :]
    eye = lax.broadcasted_iota(jnp.int32, (128, 128), 0) == lax.broadcasted_iota(jnp.int32, (128, 128), 1)
    for side, column in ((0, 0), (1, 1023)):
        values = jnp.concatenate([image[0, :, column : column + 1], image[1, :, column : column + 1]], axis=0)
        cols_send[side] = jnp.sum(jnp.where(eye, values, 0.0), axis=0, keepdims=True)
    edge = [
        copy(rows_send.at[0], rows_got.at[1], (before, b)),
        copy(rows_send.at[1], rows_got.at[0], (after, b)),
        copy(cols_send.at[0], cols_got.at[1], (w, lax.rem(b + BN - 1, BN))),
        copy(cols_send.at[1], cols_got.at[0], (w, lax.rem(b + 1, BN))),
    ]

    squared = image[0] * image[0] + image[1] * image[1]
    cubed = jnp.concatenate([squared * image[0], squared * image[1]], axis=0).astype(jnp.bfloat16)
    for n in range(4):
        pulses_here = slice(n * 256, (n + 1) * 256)
        late = slice(1024 + n * 256, 1024 + (n + 1) * 256)
        by0 = lax.dot_general(cubed, resampled[pulses_here, :], across, preferred_element_type=jnp.float32)
        by1 = lax.dot_general(cubed, resampled[late, :], across, preferred_element_type=jnp.float32)
        s0 = steer_v[0:64, pulses_here].astype(jnp.float32)
        s1 = steer_v[64:128, pulses_here].astype(jnp.float32)
        terms = s0 * (by1[:64] - by0[64:]) + s1 * (by1[64:] + by0[:64])
        summed = jnp.sum(terms, axis=0, keepdims=True)
        part_one[2 * n] = summed[:, :TILE]
        part_one[2 * n + 1] = summed[:, TILE:]
    core, half = lax.rem(b, 2), b // 2
    first_group = [(dz, dc) for dc in range(2) for dz in range(ZN) if (dz, dc) != (0, 0)]
    one = []
    for dz, dc in first_group:
        other = first_group.index(((ZN - dz) % ZN, dc))
        one.append(copy(part_one, got_one.at[other], (at(0, dz, 0), half * 2 + lax.rem(core + dc, 2))))

    for made in edge:
        made.wait_recv()
    row = lax.broadcasted_iota(jnp.int32, (64, 1024), 0)
    col = lax.broadcasted_iota(jnp.int32, (64, 1024), 1)

    def pull(d0, d1):
        inverse = lax.rsqrt(d0 * d0 + d1 * d1 + EDGE_SOFTNESS)
        return d0 * inverse, d1 * inverse

    f = [image[0], image[1]]
    above = [jnp.where(row == 0, rows_got[0, i : i + 1], pltpu.roll(f[i], 1, 0)) for i in range(2)]
    up = pull(f[0] - above[0], f[1] - above[1])
    below = [jnp.where(row == 63, rows_got[1, i : i + 1], pltpu.roll(f[i], 63, 0)) for i in range(2)]
    down = pull(f[0] - below[0], f[1] - below[1])
    beside = []
    for side in range(2):
        values = jnp.sum(jnp.where(eye, cols_got[side], 0.0), axis=1, keepdims=True)
        beside.append([values[:64], values[64:]])
    left = [jnp.where(col == 0, beside[0][i], pltpu.roll(f[i], 1, 1)) for i in range(2)]
    inward = pull(f[0] - left[0], f[1] - left[1])
    right = [jnp.where(col == 1023, beside[1][i], pltpu.roll(f[i], 1023, 1)) for i in range(2)]
    outward = pull(f[0] - right[0], f[1] - right[1])
    lower = (col > 0) | (b > 0)
    upper = (col < 1023) | (b < BN - 1)
    for i in range(2):
        total = up[i] + down[i] + jnp.where(lower, inward[i], 0.0) + jnp.where(upper, outward[i], 0.0)
        smooth[i] = f[i] - STEP_SIZE * total
    stores.append(pltpu.make_async_copy(smooth, smoothed_out, load_sem.at[3]))
    stores[1].start()

    for made in one:
        made.wait_recv()
    total = part_one[...]
    for i in range(len(first_group)):
        total = total + got_one[i]
    part_two[...] = total
    second_group = [(dh, dx, dy) for dh in range(2) for dx in range(XN) for dy in range(YN) if (dh, dx, dy) != (0, 0, 0)]
    two = []
    for dh, dx, dy in second_group:
        other = second_group.index((dh, dx, (YN - dy) % YN))
        source = part_two.at[lax.rem(x + dx, XN) * 4 + z // 2]
        two.append(copy(source, got_two.at[other], (at(dx, 0, dy), lax.rem(half + dh, 2) * 2 + core)))
    for made in two:
        made.wait_recv()
    row_sum = part_two[x * 4 + z // 2]
    for i in range(len(second_group)):
        row_sum = row_sum + got_two[i]
    offset = lax.rem(z, 2) * 64 + y * 16
    turned = pltpu.roll(jnp.broadcast_to(row_sum, (8, TILE)), lax.rem(TILE - offset, TILE), 1)
    gradient_out[...] = turned[0:1, :16] * scale

    for made in started:
        made.wait_send()
    for store in stores:
        store.wait()


def hand_on(focused, smoothed, gradient, focused_out, smoothed_out, gradient_out, held, row, sem):
    moves = [
        (src.at[q, pl.ds(h * 32, 32)], held.at[n, q, pl.ds(h * 32, 32)], dst.at[q, pl.ds(h * 32, 32)])
        for n, (src, dst) in enumerate(((focused, focused_out), (smoothed, smoothed_out)))
        for q in range(2)
        for h in range(2)
    ]
    moves.append((gradient, row, gradient_out))
    loads = [pltpu.make_async_copy(src, mid, sem.at[0, n]) for n, (src, mid, _) in enumerate(moves)]
    stores = [pltpu.make_async_copy(mid, dst, sem.at[1, n]) for n, (_, mid, dst) in enumerate(moves)]
    for made in loads:
        made.start()
    for made, store in zip(loads, stores):
        made.wait()
        store.start()
    for made in stores:
        made.wait()


def shards(pulse_data, phase_error, steering, kernel_bank, tile_offsets, kernel_ids, counts):
    bf, f32 = jnp.bfloat16, jnp.float32
    block = pltpu.VMEM((8, 16, TILE), bf)
    scratch = [block] * 24
    scratch += [pltpu.VMEM((3, 8, 16, TILE), bf)] * 8
    scratch += [pltpu.VMEM((3, 2, 4, 16, TILE), bf)] * 16
    scratch += [pltpu.VMEM((4, 4, 16, TILE), bf)] * 16
    scratch += [
        pltpu.VMEM((512, 1024), bf),
        pltpu.VMEM((2048, 1024), bf),
        pltpu.VMEM((1024, 1024), bf),
        pltpu.VMEM((128, 1024), bf),
        pltpu.VMEM((2, 64, 1024), f32),
        pltpu.VMEM((2, 64, 1024), f32),
        pltpu.VMEM((2, 2, 1024), f32),
        pltpu.VMEM((2, 2, 1024), f32),
        pltpu.VMEM((2, 1, TILE), f32),
        pltpu.VMEM((2, 1, TILE), f32),
        pltpu.VMEM((8, 1, TILE), f32),
        pltpu.VMEM((15, 8, 1, TILE), f32),
        pltpu.VMEM((8, 1, TILE), f32),
        pltpu.VMEM((15, 1, TILE), f32),
        pltpu.VMEM((64, MAXB, 64), jnp.int32),
        pltpu.VMEM((64, MAXB, 64), jnp.int32),
        pltpu.VMEM((64, 64), jnp.int32),
        pltpu.VMEM((1, 16), f32),
        pltpu.VMEM((2, 16, 1024), bf),
        pltpu.VMEM((8, 256), jnp.int32),
        pltpu.SMEM((8, 256), jnp.int32),
        pltpu.SemaphoreType.DMA((COPIES,)),
        pltpu.SemaphoreType.DMA((COPIES,)),
        pltpu.SemaphoreType.DMA((10,)),
    ]
    scale = math.sqrt(1024 / (4096 * 4096))
    image = jax.ShapeDtypeStruct((2, 64, 1024), f32)
    vmem = pl.BlockSpec(memory_space=pltpu.VMEM)
    anywhere = pl.BlockSpec(memory_space=pl.ANY)
    focused, smoothed, gradient = pl.pallas_call(
        functools.partial(kernel, scale),
        out_shape=(image, image, jax.ShapeDtypeStruct((1, 16), f32)),
        in_specs=[anywhere] * 7,
        out_specs=(anywhere, anywhere, vmem),
        scratch_shapes=scratch,
        compiler_params=pltpu.CompilerParams(
            collective_id=0, has_side_effects=True, vmem_limit_bytes=62 << 20
        ),
    )(
        jnp.transpose(tile_offsets, (0, 2, 1)),
        jnp.transpose(kernel_ids, (0, 2, 1)),
        counts,
        jnp.reshape(phase_error, (1, 16)),
        pulse_data,
        jnp.reshape(steering, (128, 1024)),
        jnp.reshape(kernel_bank, (1024, 1024)),
    )
    results = pl.pallas_call(
        hand_on,
        out_shape=(image, image, jax.ShapeDtypeStruct((1, 16), f32)),
        in_specs=[anywhere] * 3,
        out_specs=[anywhere] * 3,
        scratch_shapes=[pltpu.VMEM((2, 2, 64, 1024), f32), pltpu.VMEM((1, 16), f32), pltpu.SemaphoreType.DMA((2, 9))],
        compiler_params=pltpu.CompilerParams(vmem_limit_bytes=62 << 20),
    )(focused, smoothed, gradient)
    return results[0], results[1], jnp.reshape(results[2], (16,))


def solution(mesh):
    in_specs = (
        P(None, "wedge", "band"),
        P("wedge"),
        P(None, "wedge", None),
        P(None, None, "band"),
        P(),
        P(),
        P(),
    )
    out_specs = (P(None, "wedge", "band"), P(None, "wedge", "band"), P("wedge"))
    return jax.shard_map(shards, mesh=mesh, in_specs=in_specs, out_specs=out_specs, check_vma=False)
```

```python
import functools
import math

import jax
import jax.numpy as jnp
from jax import lax
from jax.experimental import pallas as pl
from jax.experimental.pallas import tpu as pltpu
from jax.sharding import PartitionSpec as P

TILE = 128
MAXB = 4
EDGE_SOFTNESS = 0.05
STEP_SIZE = 0.25
XN, ZN, YN, BN = 2, 8, 4, 4
MESH = pl.DeviceIdType.MESH
COPIES = 192


def kernel(scale, offsets_in, ids_in, counts_in, phase_in, pulses_in, steering, bank, focused_out, smoothed_out, gradient_out, *scratch):
    scratch = list(scratch)
    take = lambda n: [scratch.pop(0) for _ in range(n)]
    own0, pair0, own1 = take(ZN), take(ZN), take(ZN)
    column1 = take(ZN)
    y_send, y_got = take(ZN), take(ZN)
    x_send, x_got = take(ZN), take(ZN)
    lhs, resampled, bank_v, steer_v, steer_r, steer_a, steer_b, image, smooth = take(9)
    rows_send, rows_got, cols_send, cols_got = take(4)
    part_one, got_one, part_two, got_two = take(4)
    offsets, ids, counts, phase, pulses, table_v, table = take(7)
    send_sem, recv_sem, load_sem = take(3)

    w = lax.axis_index("wedge")
    b = lax.axis_index("band")
    x, z, y = w // (ZN * YN), lax.rem(w // YN, ZN), lax.rem(w, YN)

    def at(dx, dz, dy):
        return lax.rem(x + dx, XN) * (ZN * YN) + lax.rem(z + dz, ZN) * YN + lax.rem(y + dy, YN)

    def load(src, dst, n):
        made = pltpu.make_async_copy(src, dst, load_sem.at[n])
        made.start()
        return made

    first_loads = [load(pulses_in, pulses, 4), load(phase_in, phase, 5)]
    index_loads = [load(offsets_in, offsets, 6), load(ids_in, ids, 7), load(counts_in, counts, 8)]
    loads = [load(bank, bank_v, 0), load(steering, steer_v, 1)]

    wedges = XN * ZN * YN
    after, before = lax.rem(w + 1, wedges), lax.rem(w + wedges - 1, wedges)
    greeted = [(at(0, 1, 0), b), (at(0, ZN - 1, 0), b), (at(1, 0, 0), b)]
    greeted += [(at(0, 0, dy), b) for dy in range(1, YN)]
    greeted += [(w, lax.rem(b + db, BN)) for db in range(1, BN)]
    barrier = pltpu.get_barrier_semaphore()
    for device in greeted:
        pl.semaphore_signal(barrier, inc=1, device_id=device, device_id_type=MESH)

    square = lax.broadcasted_iota(jnp.int32, (16, 16), 0) == lax.broadcasted_iota(jnp.int32, (16, 16), 1)
    for made in first_loads:
        made.wait()
    angle = jnp.sum(jnp.where(square, phase[...], 0.0), axis=1, keepdims=True)
    cosine, sine = jnp.cos(angle), jnp.sin(angle)
    real, imag = pulses[0].astype(jnp.float32), pulses[1].astype(jnp.float32)
    fixed0 = (real * cosine + imag * sine).astype(jnp.bfloat16)
    fixed1 = (imag * cosine - real * sine).astype(jnp.bfloat16)
    for t in range(8):
        own0[0][t] = fixed0[:, t * TILE : (t + 1) * TILE]
        own1[0][t] = fixed1[:, t * TILE : (t + 1) * TILE]

    pl.semaphore_wait(barrier, len(greeted))

    started = []

    def copy(src, dst, device):
        index = len(started)
        made = pltpu.make_async_remote_copy(
            src, dst, send_sem.at[index], recv_sem.at[index], device_id=device, device_id_type=MESH
        )
        made.start()
        started.append(made)
        return made

    ring = {}
    own0_ring = (own0, None)
    own1_ring = (own1, None)
    pair0_ring = (pair0, None)
    column1_rings = [(column1, i) for i in range(YN - 1)]

    def part(ref, index, half):
        if index is None:
            return ref if half is None else ref.at[half]
        return ref.at[index] if half is None else ref.at[index, half]

    def send_ring(name, d, sign):
        bufs, index = name
        key = (id(bufs), index)
        half = None if d < ZN // 2 else pl.ds(0, 4) if sign > 0 else pl.ds(4, 4)
        src = part(bufs[(-sign * (d - 1)) % ZN], index, half)
        dst = part(bufs[(-sign * d) % ZN], index, half)
        ring[key, d, sign] = copy(src, dst, (at(0, sign % ZN, 0), b))

    def start_ring(name):
        for sign in (1, -1):
            send_ring(name, 1, sign)

    def take_ring(name, d):
        for sign in (1, -1):
            ring[(id(name[0]), name[1]), d, sign].wait_recv()
            if d < ZN // 2:
                send_ring(name, d + 1, sign)

    def block_at(e, dx, dy):
        return at(dx, e, dy)

    def pick(which, k, j):
        return table[which, k * MAXB + j]

    y_copies, x_copies = {}, {}

    def share_y(e):
        for dx, bufs in ((0, own0), (1, pair0)):
            k = block_at(e, dx, 0)
            for dy in range(1, YN):
                for j in range(MAXB):
                    y_send[e][dy - 1, dx, j] = bufs[e][pick(dy, k, j)]
        y_copies[e] = [
            copy(y_send[e].at[dy - 1], y_got[e].at[YN - dy - 1], (at(0, 0, dy), b)) for dy in range(1, YN)
        ]

    def share_own(e):
        k = block_at(e, 0, 0)
        for j in range(MAXB):
            x_send[e][0, j] = own1[e][pick(4, k, j)]
        x_copies[e] = [copy(x_send[e].at[0], x_got[e].at[0], (at(1, 0, 0), b))]

    def share_column(e):
        for dy in range(1, YN):
            k = block_at(e, 0, dy)
            for j in range(MAXB):
                x_send[e][dy, j] = column1[e][dy - 1, pick(4, k, j)]
        x_copies[e] += [copy(x_send[e].at[pl.ds(1, 3)], x_got[e].at[pl.ds(1, 3)], (at(1, 0, 0), b))]

    def place(row, k, loads_of):
        names = [jnp.where(j < table[6, k], pick(5, k, j), 8) for j in range(MAXB)]
        for q, load_tile in enumerate(loads_of):
            tiles = [load_tile(j).astype(jnp.float32) for j in range(MAXB)]
            summed = []
            for i in range(MAXB):
                total = tiles[i]
                for j in range(i + 1, MAXB):
                    total = total + jnp.where(names[i] == names[j], tiles[j], 0.0)
                summed.append(total.astype(jnp.bfloat16))
            here = pl.multiple_of(q * 128 + row, 16)
            for m in range(8):
                value = jnp.zeros((16, TILE), jnp.bfloat16)
                for j in reversed(range(MAXB)):
                    value = jnp.where(names[j] == m, summed[j], value)
                lhs[pl.ds(here, 16), m * TILE : (m + 1) * TILE] = value

    turns = [0, 7, 1, 6, 2, 5, 3, 4]

    def process(e):
        for made in y_copies[e] + x_copies[e]:
            made.wait_recv()

        def row_of(dx, dy):
            return lax.rem(x + dx, XN) * 64 + lax.rem(y + dy, YN) * 16

        k0, k1 = block_at(e, 0, 0), block_at(e, 1, 0)
        place(
            row_of(0, 0),
            k0,
            [lambda j: own0[e][pick(0, k0, j)], lambda j: own1[e][pick(0, k0, j)]],
        )
        place(row_of(1, 0), k1, [lambda j: pair0[e][pick(0, k1, j)], lambda j: x_got[e][0, j]])

        @pl.loop(1, YN)
        def _(dy):
            near, far = block_at(e, 0, dy), block_at(e, 1, dy)
            place(
                row_of(0, dy),
                near,
                [lambda j: y_got[e][dy - 1, 0, j], lambda j: column1[e][dy - 1, pick(0, near, j)]],
            )
            place(row_of(1, dy), far, [lambda j: y_got[e][dy - 1, 1, j], lambda j: x_got[e][dy, j]])

        place_at = turns.index(e) * 128

        @pl.loop(0, 2)
        def _(n):
            columns = pl.ds(pl.multiple_of(n * 512, 512), 512)
            got = jnp.dot(lhs[...], bank_v[:, columns], preferred_element_type=jnp.float32)
            got = got.astype(jnp.bfloat16)
            resampled[place_at : place_at + 128, columns] = got[:128]
            resampled[1024 + place_at : 1024 + place_at + 128, columns] = got[128:]

    def focus(first, last):
        inner = slice(first * 128, last * 128)
        late = slice(1024 + first * 128, 1024 + last * 128)

        for n in range(2):
            columns = slice(n * 512, (n + 1) * 512)
            by_real = jnp.dot(steer_r[:, inner], resampled[inner, columns], preferred_element_type=jnp.float32)
            by_imag = jnp.dot(steer_r[:, inner], resampled[late, columns], preferred_element_type=jnp.float32)
            real, imag = by_real[:64] - by_imag[64:], by_imag[:64] + by_real[64:]
            if first:
                real, imag = real + image[0, :, columns], imag + image[1, :, columns]
            image[0, :, columns] = real
            image[1, :, columns] = imag

    def slices(d):
        return [0] if d == 0 else [4] if d == 4 else [d, ZN - d]

    first_x = copy(own0[0], pair0[0], (at(1, 0, 0), b))
    start_ring(own0_ring)
    first_y = {
        YN - dy - 1: copy(own1[0], column1[0].at[YN - dy - 1], (at(0, 0, dy), b)) for dy in (1, YN - 1)
    }
    start_ring(own1_ring)
    first_y[1] = copy(own1[0], column1[0].at[1], (at(0, 0, 2), b))

    for made in index_loads:
        made.wait()
    near = [w] + [at(0, 0, dy) for dy in range(1, YN)] + [at(1, 0, 0), w, w]
    kind = lax.broadcasted_iota(jnp.int32, (8, wedges), 0)
    lane = lax.broadcasted_iota(jnp.int32, (8, wedges), 1)
    wanted = jnp.zeros((8, wedges), jnp.int32)
    for n, wedge in enumerate(near):
        wanted = jnp.where(kind == n, wedge, wanted)
    chosen = jnp.where(lane == wanted, 1.0, 0.0).astype(jnp.bfloat16)
    across = (((1,), (1,)), ((), ()))

    def choose(ref, rows):
        values = jnp.reshape(ref[...], (rows, wedges)).astype(jnp.float32).astype(jnp.bfloat16)
        return lax.dot_general(chosen, values, across, preferred_element_type=jnp.float32).astype(jnp.int32)

    row = lax.broadcasted_iota(jnp.int32, (8, wedges * MAXB), 0)
    picked = jnp.where(row == 5, choose(ids, wedges * MAXB), choose(offsets, wedges * MAXB))
    table_v[...] = jnp.clip(picked, 0, 7)
    table_v[6:7, 0:wedges] = choose(counts, wedges)[6:7]
    table_load = load(table_v, table, 9)
    table_load.wait()
    share_own(0)
    first_x.wait_recv()
    start_ring(pair0_ring)
    take_ring(own0_ring, 1)
    for i in (2, 0):
        first_y[i].wait_recv()
        start_ring(column1_rings[i])
    share_y(0)
    take_ring(own1_ring, 1)
    for e in slices(1):
        share_own(e)
    first_y[1].wait_recv()
    start_ring(column1_rings[1])
    share_column(0)

    loads[1].wait()
    low_half = lax.broadcasted_iota(jnp.int32, (128, TILE), 1) < 64
    for n, e in enumerate(turns):
        zz = lax.rem(z + e, ZN)
        odd = lax.rem(zz, 2)
        pieces = []
        for xx in range(XN):
            columns = pl.ds(pl.multiple_of((xx * 4 + zz // 2) * TILE, TILE), TILE)
            turn = lax.rem(odd + xx, 2) * 64
            pieces.append(pltpu.roll(steer_v[:, columns].astype(jnp.float32), turn, 1))
        piece = jnp.where(low_half, pieces[0], pieces[1])
        here = slice(n * TILE, (n + 1) * TILE)
        steer_r[:, here] = piece.astype(jnp.bfloat16)
        steer_a[here, :] = jnp.transpose(piece)
        steer_b[here, :] = jnp.transpose(jnp.concatenate([piece[64:], -piece[:64]], axis=0))

    for d in range(1, 5):
        take_ring(pair0_ring, d)
        if d < 4:
            take_ring(own0_ring, d + 1)
        for e in slices(d):
            share_y(e)
        if d >= 3:
            process(d - 2)
        for i in (2, 0):
            take_ring(column1_rings[i], d)
        if d < 4:
            take_ring(own1_ring, d + 1)
            for e in slices(d + 1):
                share_own(e)
        take_ring(column1_rings[1], d)
        for e in slices(d):
            share_column(e)
        if d == 1:
            loads[0].wait()
        if d == 4:
            focus(0, 5)
        process((ZN - (d - 1)) % ZN)
    process(3)
    focus(5, 7)
    process(4)
    focus(7, 8)
    stores = [pltpu.make_async_copy(image, focused_out, load_sem.at[2])]
    stores[0].start()

    rows_send[0] = image[:, 0, :]
    rows_send[1] = image[:, 63, :]
    eye = lax.broadcasted_iota(jnp.int32, (128, 128), 0) == lax.broadcasted_iota(jnp.int32, (128, 128), 1)
    for side, column in ((0, 0), (1, 1023)):
        values = jnp.concatenate([image[0, :, column : column + 1], image[1, :, column : column + 1]], axis=0)
        cols_send[side] = jnp.sum(jnp.where(eye, values, 0.0), axis=0, keepdims=True)
    edge = [
        copy(rows_send.at[0], rows_got.at[1], (before, b)),
        copy(rows_send.at[1], rows_got.at[0], (after, b)),
        copy(cols_send.at[0], cols_got.at[1], (w, lax.rem(b + BN - 1, BN))),
        copy(cols_send.at[1], cols_got.at[0], (w, lax.rem(b + 1, BN))),
    ]

    squared = image[0] * image[0] + image[1] * image[1]
    cubed = jnp.concatenate([squared * image[0], squared * image[1]], axis=0).astype(jnp.bfloat16)
    for n in range(4):
        inner = slice(n * 256, (n + 1) * 256)
        late = slice(1024 + n * 256, 1024 + (n + 1) * 256)
        by0 = lax.dot_general(resampled[inner, :], cubed, across, preferred_element_type=jnp.float32)
        by1 = lax.dot_general(resampled[late, :], cubed, across, preferred_element_type=jnp.float32)
        terms = jnp.sum(steer_a[inner, :] * by1 + steer_b[inner, :] * by0, axis=1, keepdims=True)
        for h in range(2):
            part = jnp.where(eye, terms[h * TILE : (h + 1) * TILE], 0.0)
            part_one[2 * n + h] = jnp.sum(part, axis=0, keepdims=True)
    core, half = lax.rem(b, 2), b // 2
    first_group = [(dz, dc) for dc in range(2) for dz in range(ZN) if (dz, dc) != (0, 0)]
    one = []
    for dz, dc in first_group:
        other = first_group.index(((ZN - dz) % ZN, dc))
        one.append(copy(part_one.at[turns.index(dz)], got_one.at[other], (at(0, dz, 0), half * 2 + lax.rem(core + dc, 2))))

    for made in edge:
        made.wait_recv()
    row = lax.broadcasted_iota(jnp.int32, (64, 1024), 0)
    col = lax.broadcasted_iota(jnp.int32, (64, 1024), 1)

    def pull(d0, d1):
        inverse = lax.rsqrt(d0 * d0 + d1 * d1 + EDGE_SOFTNESS)
        return d0 * inverse, d1 * inverse

    f = [image[0], image[1]]
    above = [jnp.where(row == 0, rows_got[0, i : i + 1], pltpu.roll(f[i], 1, 0)) for i in range(2)]
    up = pull(f[0] - above[0], f[1] - above[1])
    below = [jnp.where(row == 63, rows_got[1, i : i + 1], pltpu.roll(f[i], 63, 0)) for i in range(2)]
    down = pull(f[0] - below[0], f[1] - below[1])
    beside = []
    for side in range(2):
        values = jnp.sum(jnp.where(eye, cols_got[side], 0.0), axis=1, keepdims=True)
        beside.append([values[:64], values[64:]])
    left = [jnp.where(col == 0, beside[0][i], pltpu.roll(f[i], 1, 1)) for i in range(2)]
    inward = pull(f[0] - left[0], f[1] - left[1])
    right = [jnp.where(col == 1023, beside[1][i], pltpu.roll(f[i], 1023, 1)) for i in range(2)]
    outward = pull(f[0] - right[0], f[1] - right[1])
    lower = (col > 0) | (b > 0)
    upper = (col < 1023) | (b < BN - 1)
    for i in range(2):
        total = up[i] + down[i] + jnp.where(lower, inward[i], 0.0) + jnp.where(upper, outward[i], 0.0)
        smooth[i] = f[i] - STEP_SIZE * total
    stores.append(pltpu.make_async_copy(smooth, smoothed_out, load_sem.at[3]))
    stores[1].start()

    for made in one:
        made.wait_recv()
    total = part_one[turns.index(0)]
    for i in range(len(first_group)):
        total = total + got_one[i]
    part_two[...] = total
    second_group = [(dh, dx, dy) for dh in range(2) for dx in range(XN) for dy in range(YN) if (dh, dx, dy) != (0, 0, 0)]
    two = []
    for dh, dx, dy in second_group:
        other = second_group.index((dh, dx, (YN - dy) % YN))
        two.append(copy(part_two, got_two.at[other], (at(dx, 0, dy), lax.rem(half + dh, 2) * 2 + core)))
    for made in two:
        made.wait_recv()
    row_sum = part_two[...]
    for i in range(len(second_group)):
        row_sum = row_sum + got_two[i]
    offset = x * 64 + y * 16
    turned = pltpu.roll(jnp.broadcast_to(row_sum, (8, TILE)), lax.rem(TILE - offset, TILE), 1)
    gradient_out[...] = turned[0:1, :16] * scale

    for made in started:
        made.wait_send()
    for store in stores:
        store.wait()


def hand_on(focused, smoothed, gradient, focused_out, smoothed_out, gradient_out, held, row, sem):
    moves = [
        (src.at[q, pl.ds(h * 32, 32)], held.at[n, q, pl.ds(h * 32, 32)], dst.at[q, pl.ds(h * 32, 32)])
        for n, (src, dst) in enumerate(((focused, focused_out), (smoothed, smoothed_out)))
        for q in range(2)
        for h in range(2)
    ]
    moves.append((gradient, row, gradient_out))
    loads = [pltpu.make_async_copy(src, mid, sem.at[0, n]) for n, (src, mid, _) in enumerate(moves)]
    stores = [pltpu.make_async_copy(mid, dst, sem.at[1, n]) for n, (_, mid, dst) in enumerate(moves)]
    for made in loads:
        made.start()
    for made, store in zip(loads, stores):
        made.wait()
        store.start()
    for made in stores:
        made.wait()


def shards(pulse_data, phase_error, steering, kernel_bank, tile_offsets, kernel_ids, counts):
    bf, f32 = jnp.bfloat16, jnp.float32
    block = pltpu.VMEM((8, 16, TILE), bf)
    scratch = [block] * 24
    scratch += [pltpu.VMEM((3, 8, 16, TILE), bf)] * 8
    scratch += [pltpu.VMEM((3, 2, 4, 16, TILE), bf)] * 16
    scratch += [pltpu.VMEM((4, 4, 16, TILE), bf)] * 16
    scratch += [
        pltpu.VMEM((256, 1024), bf),
        pltpu.VMEM((2048, 1024), bf),
        pltpu.VMEM((1024, 1024), bf),
        pltpu.VMEM((128, 1024), bf),
        pltpu.VMEM((128, 1024), bf),
        pltpu.VMEM((1024, TILE), f32),
        pltpu.VMEM((1024, TILE), f32),
        pltpu.VMEM((2, 64, 1024), f32),
        pltpu.VMEM((2, 64, 1024), f32),
        pltpu.VMEM((2, 2, 1024), f32),
        pltpu.VMEM((2, 2, 1024), f32),
        pltpu.VMEM((2, 1, TILE), f32),
        pltpu.VMEM((2, 1, TILE), f32),
        pltpu.VMEM((8, 1, TILE), f32),
        pltpu.VMEM((15, 1, TILE), f32),
        pltpu.VMEM((1, TILE), f32),
        pltpu.VMEM((15, 1, TILE), f32),
        pltpu.VMEM((64, MAXB, 64), jnp.int32),
        pltpu.VMEM((64, MAXB, 64), jnp.int32),
        pltpu.VMEM((64, 64), jnp.int32),
        pltpu.VMEM((1, 16), f32),
        pltpu.VMEM((2, 16, 1024), bf),
        pltpu.VMEM((8, 256), jnp.int32),
        pltpu.SMEM((8, 256), jnp.int32),
        pltpu.SemaphoreType.DMA((COPIES,)),
        pltpu.SemaphoreType.DMA((COPIES,)),
        pltpu.SemaphoreType.DMA((10,)),
    ]
    scale = math.sqrt(1024 / (4096 * 4096))
    image = jax.ShapeDtypeStruct((2, 64, 1024), f32)
    vmem = pl.BlockSpec(memory_space=pltpu.VMEM)
    anywhere = pl.BlockSpec(memory_space=pl.ANY)
    focused, smoothed, gradient = pl.pallas_call(
        functools.partial(kernel, scale),
        out_shape=(image, image, jax.ShapeDtypeStruct((1, 16), f32)),
        in_specs=[anywhere] * 7,
        out_specs=(anywhere, anywhere, vmem),
        scratch_shapes=scratch,
        compiler_params=pltpu.CompilerParams(
            collective_id=0, has_side_effects=True, vmem_limit_bytes=62 << 20
        ),
    )(
        jnp.transpose(tile_offsets, (0, 2, 1)),
        jnp.transpose(kernel_ids, (0, 2, 1)),
        counts,
        jnp.reshape(phase_error, (1, 16)),
        pulse_data,
        jnp.reshape(steering, (128, 1024)),
        jnp.reshape(kernel_bank, (1024, 1024)),
    )
    results = pl.pallas_call(
        hand_on,
        out_shape=(image, image, jax.ShapeDtypeStruct((1, 16), f32)),
        in_specs=[anywhere] * 3,
        out_specs=[anywhere] * 3,
        scratch_shapes=[pltpu.VMEM((2, 2, 64, 1024), f32), pltpu.VMEM((1, 16), f32), pltpu.SemaphoreType.DMA((2, 9))],
        compiler_params=pltpu.CompilerParams(vmem_limit_bytes=62 << 20),
    )(focused, smoothed, gradient)
    return results[0], results[1], jnp.reshape(results[2], (16,))


def solution(mesh):
    in_specs = (
        P(None, "wedge", "band"),
        P("wedge"),
        P(None, "wedge", None),
        P(None, None, "band"),
        P(),
        P(),
        P(),
    )
    out_specs = (P(None, "wedge", "band"), P(None, "wedge", "band"), P("wedge"))
    return jax.shard_map(shards, mesh=mesh, in_specs=in_specs, out_specs=out_specs, check_vma=False)
```

```python
import functools
import math

import jax
import jax.numpy as jnp
from jax import lax
from jax.experimental import pallas as pl
from jax.experimental.pallas import tpu as pltpu
from jax.sharding import PartitionSpec as P

TILE = 128
MAXB = 4
EDGE_SOFTNESS = 0.05
STEP_SIZE = 0.25
XN, ZN, YN, BN = 2, 8, 4, 4
MESH = pl.DeviceIdType.MESH
COPIES = 192


def kernel(scale, offsets_in, ids_in, counts_in, phase_in, pulses_in, steering, bank, focused_out, smoothed_out, gradient_out, *scratch):
    scratch = list(scratch)
    take = lambda n: [scratch.pop(0) for _ in range(n)]
    own0, pair0, own1 = take(ZN), take(ZN), take(ZN)
    column1 = take(ZN)
    y_send, y_got = take(ZN), take(ZN)
    x_send, x_got = take(ZN), take(ZN)
    lhs_a, lhs_b, resampled, bank_v, steer_v, steer_r, steer_a, steer_b, image, smooth = take(10)
    rows_send, rows_got, cols_send, cols_got = take(4)
    part_one, got_one, part_two, got_two = take(4)
    offsets, ids, counts, phase, pulses, table_v, table = take(7)
    send_sem, recv_sem, load_sem = take(3)

    w = lax.axis_index("wedge")
    b = lax.axis_index("band")
    x, z, y = w // (ZN * YN), lax.rem(w // YN, ZN), lax.rem(w, YN)

    def at(dx, dz, dy):
        return lax.rem(x + dx, XN) * (ZN * YN) + lax.rem(z + dz, ZN) * YN + lax.rem(y + dy, YN)

    def load(src, dst, n):
        made = pltpu.make_async_copy(src, dst, load_sem.at[n])
        made.start()
        return made

    first_loads = [load(pulses_in, pulses, 4), load(phase_in, phase, 5)]
    index_loads = [load(offsets_in, offsets, 6), load(ids_in, ids, 7), load(counts_in, counts, 8)]
    loads = [load(bank, bank_v, 0), load(steering, steer_v, 1)]

    wedges = XN * ZN * YN
    after, before = lax.rem(w + 1, wedges), lax.rem(w + wedges - 1, wedges)
    greeted = [(at(0, 1, 0), b), (at(0, ZN - 1, 0), b), (at(1, 0, 0), b)]
    greeted += [(at(0, 0, dy), b) for dy in range(1, YN)]
    greeted += [(w, lax.rem(b + db, BN)) for db in range(1, BN)]
    barrier = pltpu.get_barrier_semaphore()
    for device in greeted:
        pl.semaphore_signal(barrier, inc=1, device_id=device, device_id_type=MESH)

    square = lax.broadcasted_iota(jnp.int32, (16, 16), 0) == lax.broadcasted_iota(jnp.int32, (16, 16), 1)
    for made in first_loads:
        made.wait()
    angle = jnp.sum(jnp.where(square, phase[...], 0.0), axis=1, keepdims=True)
    cosine, sine = jnp.cos(angle), jnp.sin(angle)
    real, imag = pulses[0].astype(jnp.float32), pulses[1].astype(jnp.float32)
    fixed0 = (real * cosine + imag * sine).astype(jnp.bfloat16)
    fixed1 = (imag * cosine - real * sine).astype(jnp.bfloat16)
    for t in range(8):
        own0[0][t] = fixed0[:, t * TILE : (t + 1) * TILE]
        own1[0][t] = fixed1[:, t * TILE : (t + 1) * TILE]

    pl.semaphore_wait(barrier, len(greeted))

    started = []

    def copy(src, dst, device):
        index = len(started)
        made = pltpu.make_async_remote_copy(
            src, dst, send_sem.at[index], recv_sem.at[index], device_id=device, device_id_type=MESH
        )
        made.start()
        started.append(made)
        return made

    ring = {}
    own0_ring = (own0, None)
    own1_ring = (own1, None)
    pair0_ring = (pair0, None)
    column1_rings = [(column1, i) for i in range(YN - 1)]

    def part(ref, index, half):
        if index is None:
            return ref if half is None else ref.at[half]
        return ref.at[index] if half is None else ref.at[index, half]

    def send_ring(name, d, sign):
        bufs, index = name
        key = (id(bufs), index)
        half = None if d < ZN // 2 else pl.ds(0, 4) if sign > 0 else pl.ds(4, 4)
        src = part(bufs[(-sign * (d - 1)) % ZN], index, half)
        dst = part(bufs[(-sign * d) % ZN], index, half)
        ring[key, d, sign] = copy(src, dst, (at(0, sign % ZN, 0), b))

    def start_ring(name):
        for sign in (1, -1):
            send_ring(name, 1, sign)

    def take_ring(name, d):
        for sign in (1, -1):
            ring[(id(name[0]), name[1]), d, sign].wait_recv()
            if d < ZN // 2:
                send_ring(name, d + 1, sign)

    def block_at(e, dx, dy):
        return at(dx, e, dy)

    def pick(which, k, j):
        return table[which, k * MAXB + j]

    y_copies, x_copies = {}, {}

    def share_y(e):
        for dx, bufs in ((0, own0), (1, pair0)):
            k = block_at(e, dx, 0)
            for dy in range(1, YN):
                for j in range(MAXB):
                    y_send[e][dy - 1, dx, j] = bufs[e][pick(dy, k, j)]
        y_copies[e] = [
            copy(y_send[e].at[dy - 1], y_got[e].at[YN - dy - 1], (at(0, 0, dy), b)) for dy in range(1, YN)
        ]

    def share_own(e):
        k = block_at(e, 0, 0)
        for j in range(MAXB):
            x_send[e][0, j] = own1[e][pick(4, k, j)]
        x_copies[e] = [copy(x_send[e].at[0], x_got[e].at[0], (at(1, 0, 0), b))]

    def share_column(e):
        for dy in range(1, YN):
            k = block_at(e, 0, dy)
            for j in range(MAXB):
                x_send[e][dy, j] = column1[e][dy - 1, pick(4, k, j)]
        x_copies[e] += [copy(x_send[e].at[pl.ds(1, 3)], x_got[e].at[pl.ds(1, 3)], (at(1, 0, 0), b))]

    def place(lhs, row, k, loads_of):
        names = [jnp.where(j < table[6, k], pick(5, k, j), 8) for j in range(MAXB)]
        for q, load_tile in loads_of:
            tiles = [load_tile(j).astype(jnp.float32) for j in range(MAXB)]
            summed = []
            for i in range(MAXB):
                total = tiles[i]
                for j in range(i + 1, MAXB):
                    total = total + jnp.where(names[i] == names[j], tiles[j], 0.0)
                summed.append(total.astype(jnp.bfloat16))
            here = pl.multiple_of(q * 128 + row, 16)
            for m in range(8):
                value = jnp.zeros((16, TILE), jnp.bfloat16)
                for j in reversed(range(MAXB)):
                    value = jnp.where(names[j] == m, summed[j], value)
                lhs[pl.ds(here, 16), m * TILE : (m + 1) * TILE] = value

    turns = [0, 7, 1, 6, 2, 5, 3, 4]

    def arrived(made):
        for one in made:
            one.wait_recv()

    def near_places(e, lhs, dx, dy):
        row = lax.rem(x + dx, XN) * 64 + lax.rem(y + dy, YN) * 16
        k = block_at(e, dx, dy)
        if dx == 0 and dy == 0:
            loads_of = [(0, lambda j: own0[e][pick(0, k, j)]), (1, lambda j: own1[e][pick(0, k, j)])]
        elif dx == 0:
            loads_of = [
                (0, lambda j: y_got[e][dy - 1, 0, j]),
                (1, lambda j: column1[e][dy - 1, pick(0, k, j)]),
            ]
        elif dy == 0:
            loads_of = [(0, lambda j: pair0[e][pick(0, k, j)]), (1, lambda j: x_got[e][0, j])]
        else:
            loads_of = [(0, lambda j: y_got[e][dy - 1, 1, j]), (1, lambda j: x_got[e][dy, j])]
        return lhs, row, k, loads_of

    def far_last(e, lhs):
        early, late = [], []
        for dx in range(XN):
            for dy in range(YN):
                lhs, row, k, loads_of = near_places(e, lhs, dx, dy)
                early.append((lhs, row, k, loads_of if dx == 0 else loads_of[:1]))
                if dx == 1:
                    late.append((lhs, row, k, loads_of[1:]))
        return early, late

    def places(e, lhs):
        return [near_places(e, lhs, dx, dy) for dx in range(XN) for dy in range(YN)]

    def product(e, lhs, beside=()):
        place_at = turns.index(e) * 128
        share = -(-len(beside) // 2)
        for n in range(2):
            columns = slice(n * 512, (n + 1) * 512)
            got = jnp.dot(lhs[...], bank_v[:, columns], preferred_element_type=jnp.float32)
            got = got.astype(jnp.bfloat16)
            resampled[place_at : place_at + 128, columns] = got[:128]
            resampled[1024 + place_at : 1024 + place_at + 128, columns] = got[128:]
            for item in beside[n * share : (n + 1) * share]:
                place(*item)

    held = lhs_a, lhs_b

    def step(position):
        e, following = turns[position], turns[position + 1]
        arrived(y_copies[following] + x_copies[following])
        product(e, held[position % 2], places(following, held[(position + 1) % 2]))

    def focus(first, last):
        inner = slice(first * 128, last * 128)
        late = slice(1024 + first * 128, 1024 + last * 128)

        for n in range(2):
            columns = slice(n * 512, (n + 1) * 512)
            by_real = jnp.dot(steer_r[:, inner], resampled[inner, columns], preferred_element_type=jnp.float32)
            by_imag = jnp.dot(steer_r[:, inner], resampled[late, columns], preferred_element_type=jnp.float32)
            real, imag = by_real[:64] - by_imag[64:], by_imag[:64] + by_real[64:]
            if first:
                real, imag = real + image[0, :, columns], imag + image[1, :, columns]
            image[0, :, columns] = real
            image[1, :, columns] = imag

    def slices(d):
        return [0] if d == 0 else [4] if d == 4 else [d, ZN - d]

    first_x = copy(own0[0], pair0[0], (at(1, 0, 0), b))
    start_ring(own0_ring)
    first_y = {
        YN - dy - 1: copy(own1[0], column1[0].at[YN - dy - 1], (at(0, 0, dy), b)) for dy in (1, YN - 1)
    }
    start_ring(own1_ring)
    first_y[1] = copy(own1[0], column1[0].at[1], (at(0, 0, 2), b))

    for made in index_loads:
        made.wait()
    near = [w] + [at(0, 0, dy) for dy in range(1, YN)] + [at(1, 0, 0), w, w]
    kind = lax.broadcasted_iota(jnp.int32, (8, wedges), 0)
    lane = lax.broadcasted_iota(jnp.int32, (8, wedges), 1)
    wanted = jnp.zeros((8, wedges), jnp.int32)
    for n, wedge in enumerate(near):
        wanted = jnp.where(kind == n, wedge, wanted)
    chosen = jnp.where(lane == wanted, 1.0, 0.0).astype(jnp.bfloat16)
    across = (((1,), (1,)), ((), ()))

    def choose(ref, rows):
        values = jnp.reshape(ref[...], (rows, wedges)).astype(jnp.float32).astype(jnp.bfloat16)
        return lax.dot_general(chosen, values, across, preferred_element_type=jnp.float32).astype(jnp.int32)

    row = lax.broadcasted_iota(jnp.int32, (8, wedges * MAXB), 0)
    picked = jnp.where(row == 5, choose(ids, wedges * MAXB), choose(offsets, wedges * MAXB))
    table_v[...] = jnp.clip(picked, 0, 7)
    table_v[6:7, 0:wedges] = choose(counts, wedges)[6:7]
    table_load = load(table_v, table, 9)
    table_load.wait()
    share_own(0)
    first_x.wait_recv()
    start_ring(pair0_ring)
    take_ring(own0_ring, 1)
    for i in (2, 0):
        first_y[i].wait_recv()
        start_ring(column1_rings[i])
    share_y(0)
    take_ring(own1_ring, 1)
    for e in slices(1):
        share_own(e)
    first_y[1].wait_recv()
    start_ring(column1_rings[1])
    share_column(0)

    loads[1].wait()
    low_half = lax.broadcasted_iota(jnp.int32, (128, TILE), 1) < 64
    for n, e in enumerate(turns):
        zz = lax.rem(z + e, ZN)
        odd = lax.rem(zz, 2)
        pieces = []
        for xx in range(XN):
            columns = pl.ds(pl.multiple_of((xx * 4 + zz // 2) * TILE, TILE), TILE)
            turn = lax.rem(odd + xx, 2) * 64
            pieces.append(pltpu.roll(steer_v[:, columns].astype(jnp.float32), turn, 1))
        piece = jnp.where(low_half, pieces[0], pieces[1])
        here = slice(n * TILE, (n + 1) * TILE)
        steer_r[:, here] = piece.astype(jnp.bfloat16)
        steer_a[here, :] = jnp.transpose(piece)
        steer_b[here, :] = jnp.transpose(jnp.concatenate([piece[64:], -piece[:64]], axis=0))

    for d in range(1, 5):
        take_ring(pair0_ring, d)
        if d < 4:
            take_ring(own0_ring, d + 1)
        for e in slices(d):
            share_y(e)
        if d >= 3:
            step(2 * d - 5)
        for i in (2, 0):
            take_ring(column1_rings[i], d)
        if d < 4:
            take_ring(own1_ring, d + 1)
            for e in slices(d + 1):
                share_own(e)
        take_ring(column1_rings[1], d)
        for e in slices(d):
            share_column(e)
        if d == 1:
            loads[0].wait()
        if d == 1:
            arrived(y_copies[0] + x_copies[0])
            for item in places(0, held[0]):
                place(*item)
        else:
            step(2 * d - 4)
    focus(0, 5)
    step(5)
    arrived(y_copies[4])
    early, late = far_last(4, held[1])
    product(3, held[0], early)
    focus(5, 7)
    arrived(x_copies[4])
    for item in late:
        place(*item)
    product(4, held[1])
    focus(7, 8)
    stores = [pltpu.make_async_copy(image, focused_out, load_sem.at[2])]
    stores[0].start()

    rows_send[0] = image[:, 0, :]
    rows_send[1] = image[:, 63, :]
    eye = lax.broadcasted_iota(jnp.int32, (128, 128), 0) == lax.broadcasted_iota(jnp.int32, (128, 128), 1)
    for side, column in ((0, 0), (1, 1023)):
        values = jnp.concatenate([image[0, :, column : column + 1], image[1, :, column : column + 1]], axis=0)
        cols_send[side] = jnp.sum(jnp.where(eye, values, 0.0), axis=0, keepdims=True)
    edge = [
        copy(rows_send.at[0], rows_got.at[1], (before, b)),
        copy(rows_send.at[1], rows_got.at[0], (after, b)),
        copy(cols_send.at[0], cols_got.at[1], (w, lax.rem(b + BN - 1, BN))),
        copy(cols_send.at[1], cols_got.at[0], (w, lax.rem(b + 1, BN))),
    ]

    squared = image[0] * image[0] + image[1] * image[1]
    cubed = jnp.concatenate([squared * image[0], squared * image[1]], axis=0).astype(jnp.bfloat16)
    for n in range(4):
        inner = slice(n * 256, (n + 1) * 256)
        late = slice(1024 + n * 256, 1024 + (n + 1) * 256)
        by0 = lax.dot_general(resampled[inner, :], cubed, across, preferred_element_type=jnp.float32)
        by1 = lax.dot_general(resampled[late, :], cubed, across, preferred_element_type=jnp.float32)
        terms = jnp.sum(steer_a[inner, :] * by1 + steer_b[inner, :] * by0, axis=1, keepdims=True)
        for h in range(2):
            part = jnp.where(eye, terms[h * TILE : (h + 1) * TILE], 0.0)
            part_one[2 * n + h] = jnp.sum(part, axis=0, keepdims=True)
    core, half = lax.rem(b, 2), b // 2
    first_group = [(dz, dc) for dc in range(2) for dz in range(ZN) if (dz, dc) != (0, 0)]
    one = []
    for dz, dc in first_group:
        other = first_group.index(((ZN - dz) % ZN, dc))
        one.append(copy(part_one.at[turns.index(dz)], got_one.at[other], (at(0, dz, 0), half * 2 + lax.rem(core + dc, 2))))

    for made in edge:
        made.wait_recv()
    row = lax.broadcasted_iota(jnp.int32, (64, 1024), 0)
    col = lax.broadcasted_iota(jnp.int32, (64, 1024), 1)

    def pull(d0, d1):
        inverse = lax.rsqrt(d0 * d0 + d1 * d1 + EDGE_SOFTNESS)
        return d0 * inverse, d1 * inverse

    f = [image[0], image[1]]
    above = [jnp.where(row == 0, rows_got[0, i : i + 1], pltpu.roll(f[i], 1, 0)) for i in range(2)]
    up = pull(f[0] - above[0], f[1] - above[1])
    below = [jnp.where(row == 63, rows_got[1, i : i + 1], pltpu.roll(f[i], 63, 0)) for i in range(2)]
    down = pull(f[0] - below[0], f[1] - below[1])
    beside = []
    for side in range(2):
        values = jnp.sum(jnp.where(eye, cols_got[side], 0.0), axis=1, keepdims=True)
        beside.append([values[:64], values[64:]])
    left = [jnp.where(col == 0, beside[0][i], pltpu.roll(f[i], 1, 1)) for i in range(2)]
    inward = pull(f[0] - left[0], f[1] - left[1])
    right = [jnp.where(col == 1023, beside[1][i], pltpu.roll(f[i], 1023, 1)) for i in range(2)]
    outward = pull(f[0] - right[0], f[1] - right[1])
    lower = (col > 0) | (b > 0)
    upper = (col < 1023) | (b < BN - 1)
    for i in range(2):
        total = up[i] + down[i] + jnp.where(lower, inward[i], 0.0) + jnp.where(upper, outward[i], 0.0)
        smooth[i] = f[i] - STEP_SIZE * total
    stores.append(pltpu.make_async_copy(smooth, smoothed_out, load_sem.at[3]))
    stores[1].start()

    for made in one:
        made.wait_recv()
    total = part_one[turns.index(0)]
    for i in range(len(first_group)):
        total = total + got_one[i]
    part_two[...] = total
    second_group = [(dh, dx, dy) for dh in range(2) for dx in range(XN) for dy in range(YN) if (dh, dx, dy) != (0, 0, 0)]
    two = []
    for dh, dx, dy in second_group:
        other = second_group.index((dh, dx, (YN - dy) % YN))
        two.append(copy(part_two, got_two.at[other], (at(dx, 0, dy), lax.rem(half + dh, 2) * 2 + core)))
    for made in two:
        made.wait_recv()
    row_sum = part_two[...]
    for i in range(len(second_group)):
        row_sum = row_sum + got_two[i]
    offset = x * 64 + y * 16
    turned = pltpu.roll(jnp.broadcast_to(row_sum, (8, TILE)), lax.rem(TILE - offset, TILE), 1)
    gradient_out[...] = turned[0:1, :16] * scale

    for made in started:
        made.wait_send()
    for store in stores:
        store.wait()


def hand_on(focused, smoothed, gradient, focused_out, smoothed_out, gradient_out, held, row, sem):
    moves = [
        (src.at[q, pl.ds(h * 32, 32)], held.at[n, q, pl.ds(h * 32, 32)], dst.at[q, pl.ds(h * 32, 32)])
        for n, (src, dst) in enumerate(((focused, focused_out), (smoothed, smoothed_out)))
        for q in range(2)
        for h in range(2)
    ]
    moves.append((gradient, row, gradient_out))
    loads = [pltpu.make_async_copy(src, mid, sem.at[0, n]) for n, (src, mid, _) in enumerate(moves)]
    stores = [pltpu.make_async_copy(mid, dst, sem.at[1, n]) for n, (_, mid, dst) in enumerate(moves)]
    for made in loads:
        made.start()
    for made, store in zip(loads, stores):
        made.wait()
        store.start()
    for made in stores:
        made.wait()


def shards(pulse_data, phase_error, steering, kernel_bank, tile_offsets, kernel_ids, counts):
    bf, f32 = jnp.bfloat16, jnp.float32
    block = pltpu.VMEM((8, 16, TILE), bf)
    scratch = [block] * 24
    scratch += [pltpu.VMEM((3, 8, 16, TILE), bf)] * 8
    scratch += [pltpu.VMEM((3, 2, 4, 16, TILE), bf)] * 16
    scratch += [pltpu.VMEM((4, 4, 16, TILE), bf)] * 16
    scratch += [
        pltpu.VMEM((256, 1024), bf),
        pltpu.VMEM((256, 1024), bf),
        pltpu.VMEM((2048, 1024), bf),
        pltpu.VMEM((1024, 1024), bf),
        pltpu.VMEM((128, 1024), bf),
        pltpu.VMEM((128, 1024), bf),
        pltpu.VMEM((1024, TILE), f32),
        pltpu.VMEM((1024, TILE), f32),
        pltpu.VMEM((2, 64, 1024), f32),
        pltpu.VMEM((2, 64, 1024), f32),
        pltpu.VMEM((2, 2, 1024), f32),
        pltpu.VMEM((2, 2, 1024), f32),
        pltpu.VMEM((2, 1, TILE), f32),
        pltpu.VMEM((2, 1, TILE), f32),
        pltpu.VMEM((8, 1, TILE), f32),
        pltpu.VMEM((15, 1, TILE), f32),
        pltpu.VMEM((1, TILE), f32),
        pltpu.VMEM((15, 1, TILE), f32),
        pltpu.VMEM((64, MAXB, 64), jnp.int32),
        pltpu.VMEM((64, MAXB, 64), jnp.int32),
        pltpu.VMEM((64, 64), jnp.int32),
        pltpu.VMEM((1, 16), f32),
        pltpu.VMEM((2, 16, 1024), bf),
        pltpu.VMEM((8, 256), jnp.int32),
        pltpu.SMEM((8, 256), jnp.int32),
        pltpu.SemaphoreType.DMA((COPIES,)),
        pltpu.SemaphoreType.DMA((COPIES,)),
        pltpu.SemaphoreType.DMA((10,)),
    ]
    scale = math.sqrt(1024 / (4096 * 4096))
    image = jax.ShapeDtypeStruct((2, 64, 1024), f32)
    vmem = pl.BlockSpec(memory_space=pltpu.VMEM)
    anywhere = pl.BlockSpec(memory_space=pl.ANY)
    focused, smoothed, gradient = pl.pallas_call(
        functools.partial(kernel, scale),
        out_shape=(image, image, jax.ShapeDtypeStruct((1, 16), f32)),
        in_specs=[anywhere] * 7,
        out_specs=(anywhere, anywhere, vmem),
        scratch_shapes=scratch,
        compiler_params=pltpu.CompilerParams(
            collective_id=0, has_side_effects=True, vmem_limit_bytes=62 << 20
        ),
    )(
        jnp.transpose(tile_offsets, (0, 2, 1)),
        jnp.transpose(kernel_ids, (0, 2, 1)),
        counts,
        jnp.reshape(phase_error, (1, 16)),
        pulse_data,
        jnp.reshape(steering, (128, 1024)),
        jnp.reshape(kernel_bank, (1024, 1024)),
    )
    results = pl.pallas_call(
        hand_on,
        out_shape=(image, image, jax.ShapeDtypeStruct((1, 16), f32)),
        in_specs=[anywhere] * 3,
        out_specs=[anywhere] * 3,
        scratch_shapes=[pltpu.VMEM((2, 2, 64, 1024), f32), pltpu.VMEM((1, 16), f32), pltpu.SemaphoreType.DMA((2, 9))],
        compiler_params=pltpu.CompilerParams(vmem_limit_bytes=62 << 20),
    )(focused, smoothed, gradient)
    return results[0], results[1], jnp.reshape(results[2], (16,))


def solution(mesh):
    in_specs = (
        P(None, "wedge", "band"),
        P("wedge"),
        P(None, "wedge", None),
        P(None, None, "band"),
        P(),
        P(),
        P(),
    )
    out_specs = (P(None, "wedge", "band"), P(None, "wedge", "band"), P("wedge"))
    return jax.shard_map(shards, mesh=mesh, in_specs=in_specs, out_specs=out_specs, check_vma=False)
```

```python
import functools
import math

import jax
import jax.numpy as jnp
from jax import lax
from jax.experimental import pallas as pl
from jax.experimental.pallas import tpu as pltpu
from jax.sharding import PartitionSpec as P

TILE = 128
MAXB = 4
EDGE_SOFTNESS = 0.05
STEP_SIZE = 0.25
XN, ZN, YN, BN = 2, 8, 4, 4
MESH = pl.DeviceIdType.MESH
COPIES = 192


def kernel(scale, offsets_in, ids_in, counts_in, phase_in, pulses_in, steering, bank, focused_out, smoothed_out, gradient_out, *scratch):
    scratch = list(scratch)
    take = lambda n: [scratch.pop(0) for _ in range(n)]
    own0, pair0, own1 = take(ZN), take(ZN), take(ZN)
    column1 = take(ZN)
    y_send, y_got = take(ZN), take(ZN)
    x_send, x_got = take(ZN), take(ZN)
    lhs_a, lhs_b, resampled, bank_v, steer_v, steer_r, steer_a, steer_b, image, smooth = take(10)
    rows_send, rows_got, cols_send, cols_got = take(4)
    part_one, got_one, part_two, got_two = take(4)
    offsets, ids, counts, phase, pulses, table_v, table = take(7)
    send_sem, recv_sem, load_sem = take(3)

    w = lax.axis_index("wedge")
    b = lax.axis_index("band")
    x, z, y = w // (ZN * YN), lax.rem(w // YN, ZN), lax.rem(w, YN)

    def at(dx, dz, dy):
        return lax.rem(x + dx, XN) * (ZN * YN) + lax.rem(z + dz, ZN) * YN + lax.rem(y + dy, YN)

    def load(src, dst, n):
        made = pltpu.make_async_copy(src, dst, load_sem.at[n])
        made.start()
        return made

    first_loads = [load(pulses_in, pulses, 4), load(phase_in, phase, 5)]
    index_loads = [load(offsets_in, offsets, 6), load(ids_in, ids, 7), load(counts_in, counts, 8)]
    loads = [load(bank, bank_v, 0), load(steering, steer_v, 1)]

    wedges = XN * ZN * YN
    after, before = lax.rem(w + 1, wedges), lax.rem(w + wedges - 1, wedges)
    greeted = [(at(0, 1, 0), b), (at(0, ZN - 1, 0), b), (at(1, 0, 0), b)]
    greeted += [(at(0, 0, dy), b) for dy in range(1, YN)]
    greeted += [(w, lax.rem(b + db, BN)) for db in range(1, BN)]
    barrier = pltpu.get_barrier_semaphore()
    for device in greeted:
        pl.semaphore_signal(barrier, inc=1, device_id=device, device_id_type=MESH)

    square = lax.broadcasted_iota(jnp.int32, (16, 16), 0) == lax.broadcasted_iota(jnp.int32, (16, 16), 1)
    for made in first_loads:
        made.wait()
    angle = jnp.sum(jnp.where(square, phase[...], 0.0), axis=1, keepdims=True)
    cosine, sine = jnp.cos(angle), jnp.sin(angle)
    real, imag = pulses[0].astype(jnp.float32), pulses[1].astype(jnp.float32)
    fixed0 = (real * cosine + imag * sine).astype(jnp.bfloat16)
    fixed1 = (imag * cosine - real * sine).astype(jnp.bfloat16)
    for t in range(8):
        own0[0][t] = fixed0[:, t * TILE : (t + 1) * TILE]
        own1[0][t] = fixed1[:, t * TILE : (t + 1) * TILE]

    pl.semaphore_wait(barrier, len(greeted))

    started = []

    def copy(src, dst, device):
        index = len(started)
        made = pltpu.make_async_remote_copy(
            src, dst, send_sem.at[index], recv_sem.at[index], device_id=device, device_id_type=MESH
        )
        made.start()
        started.append(made)
        return made

    ring = {}
    own0_ring = (own0, None)
    own1_ring = (own1, None)
    pair0_ring = (pair0, None)
    column1_rings = [(column1, i) for i in range(YN - 1)]

    def part(ref, index, half):
        if index is None:
            return ref if half is None else ref.at[half]
        return ref.at[index] if half is None else ref.at[index, half]

    def send_ring(name, d, sign):
        bufs, index = name
        key = (id(bufs), index)
        half = None if d < ZN // 2 else pl.ds(0, 4) if sign > 0 else pl.ds(4, 4)
        src = part(bufs[(-sign * (d - 1)) % ZN], index, half)
        dst = part(bufs[(-sign * d) % ZN], index, half)
        ring[key, d, sign] = copy(src, dst, (at(0, sign % ZN, 0), b))

    def start_ring(name):
        for sign in (1, -1):
            send_ring(name, 1, sign)

    def take_ring(name, d):
        for sign in (1, -1):
            ring[(id(name[0]), name[1]), d, sign].wait_recv()
            if d < ZN // 2:
                send_ring(name, d + 1, sign)

    def block_at(e, dx, dy):
        return at(dx, e, dy)

    def pick(which, k, j):
        return table[which, k * MAXB + j]

    y_copies, x_copies = {}, {}

    def share_y(e):
        for dx, bufs in ((0, own0), (1, pair0)):
            k = block_at(e, dx, 0)
            for dy in range(1, YN):
                for j in range(MAXB):
                    y_send[e][dy - 1, dx, j] = bufs[e][pick(dy, k, j)]
        y_copies[e] = [
            copy(y_send[e].at[dy - 1], y_got[e].at[YN - dy - 1], (at(0, 0, dy), b)) for dy in range(1, YN)
        ]

    def share_own(e):
        k = block_at(e, 0, 0)
        for j in range(MAXB):
            x_send[e][0, j] = own1[e][pick(4, k, j)]
        x_copies[e] = [copy(x_send[e].at[0], x_got[e].at[0], (at(1, 0, 0), b))]

    def share_column(e):
        for dy in range(1, YN):
            k = block_at(e, 0, dy)
            for j in range(MAXB):
                x_send[e][dy, j] = column1[e][dy - 1, pick(4, k, j)]
        x_copies[e] += [copy(x_send[e].at[pl.ds(1, 3)], x_got[e].at[pl.ds(1, 3)], (at(1, 0, 0), b))]

    def place(lhs, row, k, loads_of):
        names = [jnp.where(j < table[6, k], pick(5, k, j), 8) for j in range(MAXB)]
        for q, load_tile in loads_of:
            tiles = [load_tile(j).astype(jnp.float32) for j in range(MAXB)]
            summed = []
            for i in range(MAXB):
                total = tiles[i]
                for j in range(i + 1, MAXB):
                    total = total + jnp.where(names[i] == names[j], tiles[j], 0.0)
                summed.append(total.astype(jnp.bfloat16))
            here = pl.multiple_of(q * 128 + row, 16)
            for m in range(8):
                value = jnp.zeros((16, TILE), jnp.bfloat16)
                for j in reversed(range(MAXB)):
                    value = jnp.where(names[j] == m, summed[j], value)
                lhs[pl.ds(here, 16), m * TILE : (m + 1) * TILE] = value

    turns = [0, 7, 1, 6, 2, 5, 3, 4]

    def arrived(made):
        for one in made:
            one.wait_recv()

    def near_places(e, lhs, dx, dy):
        row = lax.rem(x + dx, XN) * 64 + lax.rem(y + dy, YN) * 16
        k = block_at(e, dx, dy)
        if dx == 0 and dy == 0:
            loads_of = [(0, lambda j: own0[e][pick(0, k, j)]), (1, lambda j: own1[e][pick(0, k, j)])]
        elif dx == 0:
            loads_of = [
                (0, lambda j: y_got[e][dy - 1, 0, j]),
                (1, lambda j: column1[e][dy - 1, pick(0, k, j)]),
            ]
        elif dy == 0:
            loads_of = [(0, lambda j: pair0[e][pick(0, k, j)]), (1, lambda j: x_got[e][0, j])]
        else:
            loads_of = [(0, lambda j: y_got[e][dy - 1, 1, j]), (1, lambda j: x_got[e][dy, j])]
        return lhs, row, k, loads_of

    def far_last(e, lhs):
        early, late = [], []
        for dx in range(XN):
            for dy in range(YN):
                lhs, row, k, loads_of = near_places(e, lhs, dx, dy)
                early.append((lhs, row, k, loads_of if dx == 0 else loads_of[:1]))
                if dx == 1:
                    late.append((lhs, row, k, loads_of[1:]))
        return early, late

    def places(e, lhs):
        return [near_places(e, lhs, dx, dy) for dx in range(XN) for dy in range(YN)]

    def product(e, lhs, beside=()):
        place_at = turns.index(e) * 128
        share = -(-len(beside) // 2)
        for n in range(2):
            columns = slice(n * 512, (n + 1) * 512)
            got = jnp.dot(lhs[...], bank_v[:, columns], preferred_element_type=jnp.float32)
            got = got.astype(jnp.bfloat16)
            resampled[place_at : place_at + 128, columns] = got[:128]
            resampled[1024 + place_at : 1024 + place_at + 128, columns] = got[128:]
            for item in beside[n * share : (n + 1) * share]:
                place(*item)

    held = lhs_a, lhs_b

    def step(position):
        e, following = turns[position], turns[position + 1]
        arrived(y_copies[following] + x_copies[following])
        product(e, held[position % 2], places(following, held[(position + 1) % 2]))

    def focus(first, last):
        inner = slice(first * 128, last * 128)
        late = slice(1024 + first * 128, 1024 + last * 128)

        for n in range(2):
            columns = slice(n * 512, (n + 1) * 512)
            by_real = jnp.dot(steer_r[:, inner], resampled[inner, columns], preferred_element_type=jnp.float32)
            by_imag = jnp.dot(steer_r[:, inner], resampled[late, columns], preferred_element_type=jnp.float32)
            real, imag = by_real[:64] - by_imag[64:], by_imag[:64] + by_real[64:]
            if first:
                real, imag = real + image[0, :, columns], imag + image[1, :, columns]
            image[0, :, columns] = real
            image[1, :, columns] = imag

    def slices(d):
        return [0] if d == 0 else [4] if d == 4 else [d, ZN - d]

    first_x = copy(own0[0], pair0[0], (at(1, 0, 0), b))
    start_ring(own0_ring)
    first_y = {
        YN - dy - 1: copy(own1[0], column1[0].at[YN - dy - 1], (at(0, 0, dy), b)) for dy in (1, YN - 1)
    }
    start_ring(own1_ring)
    first_y[1] = copy(own1[0], column1[0].at[1], (at(0, 0, 2), b))

    for made in index_loads:
        made.wait()
    near = [w] + [at(0, 0, dy) for dy in range(1, YN)] + [at(1, 0, 0), w, w]
    kind = lax.broadcasted_iota(jnp.int32, (8, wedges), 0)
    lane = lax.broadcasted_iota(jnp.int32, (8, wedges), 1)
    wanted = jnp.zeros((8, wedges), jnp.int32)
    for n, wedge in enumerate(near):
        wanted = jnp.where(kind == n, wedge, wanted)
    chosen = jnp.where(lane == wanted, 1.0, 0.0).astype(jnp.bfloat16)
    across = (((1,), (1,)), ((), ()))

    def choose(ref, rows):
        values = jnp.reshape(ref[...], (rows, wedges)).astype(jnp.float32).astype(jnp.bfloat16)
        return lax.dot_general(chosen, values, across, preferred_element_type=jnp.float32).astype(jnp.int32)

    row = lax.broadcasted_iota(jnp.int32, (8, wedges * MAXB), 0)
    picked = jnp.where(row == 5, choose(ids, wedges * MAXB), choose(offsets, wedges * MAXB))
    table_v[...] = jnp.clip(picked, 0, 7)
    table_v[6:7, 0:wedges] = choose(counts, wedges)[6:7]
    table_load = load(table_v, table, 9)
    first_x.wait_recv()
    start_ring(pair0_ring)
    take_ring(own0_ring, 1)
    for i in (2, 0):
        first_y[i].wait_recv()
        start_ring(column1_rings[i])
    table_load.wait()
    share_own(0)
    share_y(0)
    take_ring(own1_ring, 1)
    for e in slices(1):
        share_own(e)
    first_y[1].wait_recv()
    start_ring(column1_rings[1])
    share_column(0)

    loads[1].wait()
    low_half = lax.broadcasted_iota(jnp.int32, (128, TILE), 1) < 64
    for n, e in enumerate(turns):
        zz = lax.rem(z + e, ZN)
        odd = lax.rem(zz, 2)
        pieces = []
        for xx in range(XN):
            columns = pl.ds(pl.multiple_of((xx * 4 + zz // 2) * TILE, TILE), TILE)
            turn = lax.rem(odd + xx, 2) * 64
            pieces.append(pltpu.roll(steer_v[:, columns].astype(jnp.float32), turn, 1))
        piece = jnp.where(low_half, pieces[0], pieces[1])
        here = slice(n * TILE, (n + 1) * TILE)
        steer_r[:, here] = piece.astype(jnp.bfloat16)
        steer_a[here, :] = jnp.transpose(piece)
        steer_b[here, :] = jnp.transpose(jnp.concatenate([piece[64:], -piece[:64]], axis=0))

    for d in range(1, 5):
        take_ring(pair0_ring, d)
        if d < 4:
            take_ring(own0_ring, d + 1)
        for e in slices(d):
            share_y(e)
        if d >= 3:
            step(2 * d - 5)
        for i in (2, 0):
            take_ring(column1_rings[i], d)
        if d < 4:
            take_ring(own1_ring, d + 1)
            for e in slices(d + 1):
                share_own(e)
        take_ring(column1_rings[1], d)
        for e in slices(d):
            share_column(e)
        if d == 1:
            loads[0].wait()
        if d == 1:
            arrived(y_copies[0] + x_copies[0])
            for item in places(0, held[0]):
                place(*item)
        else:
            step(2 * d - 4)
    focus(0, 5)
    step(5)
    arrived(y_copies[4])
    early, late = far_last(4, held[1])
    product(3, held[0], early)
    focus(5, 7)
    arrived(x_copies[4])
    for item in late:
        place(*item)
    product(4, held[1])
    focus(7, 8)
    stores = [pltpu.make_async_copy(image, focused_out, load_sem.at[2])]
    stores[0].start()

    rows_send[0] = image[:, 0, :]
    rows_send[1] = image[:, 63, :]
    eye = lax.broadcasted_iota(jnp.int32, (128, 128), 0) == lax.broadcasted_iota(jnp.int32, (128, 128), 1)
    for side, column in ((0, 0), (1, 1023)):
        values = jnp.concatenate([image[0, :, column : column + 1], image[1, :, column : column + 1]], axis=0)
        cols_send[side] = jnp.sum(jnp.where(eye, values, 0.0), axis=0, keepdims=True)
    edge = [
        copy(rows_send.at[0], rows_got.at[1], (before, b)),
        copy(rows_send.at[1], rows_got.at[0], (after, b)),
        copy(cols_send.at[0], cols_got.at[1], (w, lax.rem(b + BN - 1, BN))),
        copy(cols_send.at[1], cols_got.at[0], (w, lax.rem(b + 1, BN))),
    ]

    squared = image[0] * image[0] + image[1] * image[1]
    cubed = jnp.concatenate([squared * image[0], squared * image[1]], axis=0).astype(jnp.bfloat16)
    for n in range(4):
        inner = slice(n * 256, (n + 1) * 256)
        late = slice(1024 + n * 256, 1024 + (n + 1) * 256)
        by0 = lax.dot_general(resampled[inner, :], cubed, across, preferred_element_type=jnp.float32)
        by1 = lax.dot_general(resampled[late, :], cubed, across, preferred_element_type=jnp.float32)
        terms = jnp.sum(steer_a[inner, :] * by1 + steer_b[inner, :] * by0, axis=1, keepdims=True)
        for h in range(2):
            part = jnp.where(eye, terms[h * TILE : (h + 1) * TILE], 0.0)
            part_one[2 * n + h] = jnp.sum(part, axis=0, keepdims=True)
    core, half = lax.rem(b, 2), b // 2
    first_group = [(dz, dc) for dc in range(2) for dz in range(ZN) if (dz, dc) != (0, 0)]
    one = []
    for dz, dc in first_group:
        other = first_group.index(((ZN - dz) % ZN, dc))
        one.append(copy(part_one.at[turns.index(dz)], got_one.at[other], (at(0, dz, 0), half * 2 + lax.rem(core + dc, 2))))

    for made in edge:
        made.wait_recv()
    row = lax.broadcasted_iota(jnp.int32, (64, 1024), 0)
    col = lax.broadcasted_iota(jnp.int32, (64, 1024), 1)

    def pull(d0, d1):
        inverse = lax.rsqrt(d0 * d0 + d1 * d1 + EDGE_SOFTNESS)
        return d0 * inverse, d1 * inverse

    f = [image[0], image[1]]
    above = [jnp.where(row == 0, rows_got[0, i : i + 1], pltpu.roll(f[i], 1, 0)) for i in range(2)]
    up = pull(f[0] - above[0], f[1] - above[1])
    below = [jnp.where(row == 63, rows_got[1, i : i + 1], pltpu.roll(f[i], 63, 0)) for i in range(2)]
    down = pull(f[0] - below[0], f[1] - below[1])
    beside = []
    for side in range(2):
        values = jnp.sum(jnp.where(eye, cols_got[side], 0.0), axis=1, keepdims=True)
        beside.append([values[:64], values[64:]])
    left = [jnp.where(col == 0, beside[0][i], pltpu.roll(f[i], 1, 1)) for i in range(2)]
    inward = pull(f[0] - left[0], f[1] - left[1])
    right = [jnp.where(col == 1023, beside[1][i], pltpu.roll(f[i], 1023, 1)) for i in range(2)]
    outward = pull(f[0] - right[0], f[1] - right[1])
    lower = (col > 0) | (b > 0)
    upper = (col < 1023) | (b < BN - 1)
    for i in range(2):
        total = up[i] + down[i] + jnp.where(lower, inward[i], 0.0) + jnp.where(upper, outward[i], 0.0)
        smooth[i] = f[i] - STEP_SIZE * total
    stores.append(pltpu.make_async_copy(smooth, smoothed_out, load_sem.at[3]))
    stores[1].start()

    for made in one:
        made.wait_recv()
    total = part_one[turns.index(0)]
    for i in range(len(first_group)):
        total = total + got_one[i]
    part_two[...] = total
    second_group = [(dh, dx, dy) for dh in range(2) for dx in range(XN) for dy in range(YN) if (dh, dx, dy) != (0, 0, 0)]
    two = []
    for dh, dx, dy in second_group:
        other = second_group.index((dh, dx, (YN - dy) % YN))
        two.append(copy(part_two, got_two.at[other], (at(dx, 0, dy), lax.rem(half + dh, 2) * 2 + core)))
    for made in two:
        made.wait_recv()
    row_sum = part_two[...]
    for i in range(len(second_group)):
        row_sum = row_sum + got_two[i]
    offset = x * 64 + y * 16
    turned = pltpu.roll(jnp.broadcast_to(row_sum, (8, TILE)), lax.rem(TILE - offset, TILE), 1)
    gradient_out[...] = turned[0:1, :16] * scale

    for made in started:
        made.wait_send()
    for store in stores:
        store.wait()


def hand_on(focused, smoothed, gradient, focused_out, smoothed_out, gradient_out, held, row, sem):
    moves = [
        (src.at[q, pl.ds(h * 32, 32)], held.at[n, q, pl.ds(h * 32, 32)], dst.at[q, pl.ds(h * 32, 32)])
        for n, (src, dst) in enumerate(((focused, focused_out), (smoothed, smoothed_out)))
        for q in range(2)
        for h in range(2)
    ]
    moves.append((gradient, row, gradient_out))
    loads = [pltpu.make_async_copy(src, mid, sem.at[0, n]) for n, (src, mid, _) in enumerate(moves)]
    stores = [pltpu.make_async_copy(mid, dst, sem.at[1, n]) for n, (_, mid, dst) in enumerate(moves)]
    for made in loads:
        made.start()
    for made, store in zip(loads, stores):
        made.wait()
        store.start()
    for made in stores:
        made.wait()


def shards(pulse_data, phase_error, steering, kernel_bank, tile_offsets, kernel_ids, counts):
    bf, f32 = jnp.bfloat16, jnp.float32
    block = pltpu.VMEM((8, 16, TILE), bf)
    scratch = [block] * 24
    scratch += [pltpu.VMEM((3, 8, 16, TILE), bf)] * 8
    scratch += [pltpu.VMEM((3, 2, 4, 16, TILE), bf)] * 16
    scratch += [pltpu.VMEM((4, 4, 16, TILE), bf)] * 16
    scratch += [
        pltpu.VMEM((256, 1024), bf),
        pltpu.VMEM((256, 1024), bf),
        pltpu.VMEM((2048, 1024), bf),
        pltpu.VMEM((1024, 1024), bf),
        pltpu.VMEM((128, 1024), bf),
        pltpu.VMEM((128, 1024), bf),
        pltpu.VMEM((1024, TILE), f32),
        pltpu.VMEM((1024, TILE), f32),
        pltpu.VMEM((2, 64, 1024), f32),
        pltpu.VMEM((2, 64, 1024), f32),
        pltpu.VMEM((2, 2, 1024), f32),
        pltpu.VMEM((2, 2, 1024), f32),
        pltpu.VMEM((2, 1, TILE), f32),
        pltpu.VMEM((2, 1, TILE), f32),
        pltpu.VMEM((8, 1, TILE), f32),
        pltpu.VMEM((15, 1, TILE), f32),
        pltpu.VMEM((1, TILE), f32),
        pltpu.VMEM((15, 1, TILE), f32),
        pltpu.VMEM((64, MAXB, 64), jnp.int32),
        pltpu.VMEM((64, MAXB, 64), jnp.int32),
        pltpu.VMEM((64, 64), jnp.int32),
        pltpu.VMEM((1, 16), f32),
        pltpu.VMEM((2, 16, 1024), bf),
        pltpu.VMEM((8, 256), jnp.int32),
        pltpu.SMEM((8, 256), jnp.int32),
        pltpu.SemaphoreType.DMA((COPIES,)),
        pltpu.SemaphoreType.DMA((COPIES,)),
        pltpu.SemaphoreType.DMA((10,)),
    ]
    scale = math.sqrt(1024 / (4096 * 4096))
    image = jax.ShapeDtypeStruct((2, 64, 1024), f32)
    vmem = pl.BlockSpec(memory_space=pltpu.VMEM)
    anywhere = pl.BlockSpec(memory_space=pl.ANY)
    focused, smoothed, gradient = pl.pallas_call(
        functools.partial(kernel, scale),
        out_shape=(image, image, jax.ShapeDtypeStruct((1, 16), f32)),
        in_specs=[anywhere] * 7,
        out_specs=(anywhere, anywhere, vmem),
        scratch_shapes=scratch,
        compiler_params=pltpu.CompilerParams(
            collective_id=0, has_side_effects=True, vmem_limit_bytes=62 << 20
        ),
    )(
        jnp.transpose(tile_offsets, (0, 2, 1)),
        jnp.transpose(kernel_ids, (0, 2, 1)),
        counts,
        jnp.reshape(phase_error, (1, 16)),
        pulse_data,
        jnp.reshape(steering, (128, 1024)),
        jnp.reshape(kernel_bank, (1024, 1024)),
    )
    results = pl.pallas_call(
        hand_on,
        out_shape=(image, image, jax.ShapeDtypeStruct((1, 16), f32)),
        in_specs=[anywhere] * 3,
        out_specs=[anywhere] * 3,
        scratch_shapes=[pltpu.VMEM((2, 2, 64, 1024), f32), pltpu.VMEM((1, 16), f32), pltpu.SemaphoreType.DMA((2, 9))],
        compiler_params=pltpu.CompilerParams(vmem_limit_bytes=62 << 20),
    )(focused, smoothed, gradient)
    return results[0], results[1], jnp.reshape(results[2], (16,))


def solution(mesh):
    in_specs = (
        P(None, "wedge", "band"),
        P("wedge"),
        P(None, "wedge", None),
        P(None, None, "band"),
        P(),
        P(),
        P(),
    )
    out_specs = (P(None, "wedge", "band"), P(None, "wedge", "band"), P("wedge"))
    return jax.shard_map(shards, mesh=mesh, in_specs=in_specs, out_specs=out_specs, check_vma=False)
```

```python
import functools
import math

import jax
import jax.numpy as jnp
from jax import lax
from jax.experimental import pallas as pl
from jax.experimental.pallas import tpu as pltpu
from jax.sharding import PartitionSpec as P

TILE = 128
MAXB = 4
EDGE_SOFTNESS = 0.05
STEP_SIZE = 0.25
XN, ZN, YN, BN = 2, 8, 4, 4
MESH = pl.DeviceIdType.MESH
COPIES = 192


def kernel(scale, offsets_in, ids_in, counts_in, phase_in, pulses_in, steering, bank, focused_out, smoothed_out, gradient_out, *scratch):
    scratch = list(scratch)
    take = lambda n: [scratch.pop(0) for _ in range(n)]
    own0, pair0, own1 = take(ZN), take(ZN), take(ZN)
    column1 = take(ZN)
    y_send, y_got = take(ZN), take(ZN)
    x_send, x_got = take(ZN), take(ZN)
    lhs_a, lhs_b, resampled, bank_v, steer_v, steer_r, steer_a, steer_b, image, smooth = take(10)
    rows_send, rows_got, cols_send, cols_got = take(4)
    part_one, got_one, part_two, got_two = take(4)
    offsets, ids, counts, phase, pulses, table_v, table = take(7)
    send_sem, recv_sem, load_sem = take(3)

    w = lax.axis_index("wedge")
    b = lax.axis_index("band")
    x, z, y = w // (ZN * YN), lax.rem(w // YN, ZN), lax.rem(w, YN)

    def at(dx, dz, dy):
        return lax.rem(x + dx, XN) * (ZN * YN) + lax.rem(z + dz, ZN) * YN + lax.rem(y + dy, YN)

    def load(src, dst, n):
        made = pltpu.make_async_copy(src, dst, load_sem.at[n])
        made.start()
        return made

    first_loads = [load(pulses_in, pulses, 4), load(phase_in, phase, 5)]
    index_loads = [load(offsets_in, offsets, 6), load(ids_in, ids, 7), load(counts_in, counts, 8)]
    loads = [load(bank, bank_v, 0), load(steering, steer_v, 1)]

    wedges = XN * ZN * YN
    after, before = lax.rem(w + 1, wedges), lax.rem(w + wedges - 1, wedges)
    greeted = [(at(0, 1, 0), b), (at(0, ZN - 1, 0), b), (at(1, 0, 0), b)]
    greeted += [(at(0, 0, dy), b) for dy in range(1, YN)]
    greeted += [(w, lax.rem(b + db, BN)) for db in range(1, BN)]
    barrier = pltpu.get_barrier_semaphore()
    for device in greeted:
        pl.semaphore_signal(barrier, inc=1, device_id=device, device_id_type=MESH)

    square = lax.broadcasted_iota(jnp.int32, (16, 16), 0) == lax.broadcasted_iota(jnp.int32, (16, 16), 1)
    for made in first_loads:
        made.wait()
    angle = jnp.sum(jnp.where(square, phase[...], 0.0), axis=1, keepdims=True)
    cosine, sine = jnp.cos(angle), jnp.sin(angle)
    real, imag = pulses[0].astype(jnp.float32), pulses[1].astype(jnp.float32)
    fixed0 = (real * cosine + imag * sine).astype(jnp.bfloat16)
    fixed1 = (imag * cosine - real * sine).astype(jnp.bfloat16)
    for t in range(8):
        own0[0][t] = fixed0[:, t * TILE : (t + 1) * TILE]
        own1[0][t] = fixed1[:, t * TILE : (t + 1) * TILE]

    pl.semaphore_wait(barrier, len(greeted))

    started = []

    def copy(src, dst, device):
        index = len(started)
        made = pltpu.make_async_remote_copy(
            src, dst, send_sem.at[index], recv_sem.at[index], device_id=device, device_id_type=MESH
        )
        made.start()
        started.append(made)
        return made

    ring = {}
    own0_ring = (own0, None)
    own1_ring = (own1, None)
    pair0_ring = (pair0, None)
    column1_rings = [(column1, i) for i in range(YN - 1)]

    def part(ref, index, half):
        if index is None:
            return ref if half is None else ref.at[half]
        return ref.at[index] if half is None else ref.at[index, half]

    def send_ring(name, d, sign):
        bufs, index = name
        key = (id(bufs), index)
        half = None if d < ZN // 2 else pl.ds(0, 4) if sign > 0 else pl.ds(4, 4)
        src = part(bufs[(-sign * (d - 1)) % ZN], index, half)
        dst = part(bufs[(-sign * d) % ZN], index, half)
        ring[key, d, sign] = copy(src, dst, (at(0, sign % ZN, 0), b))

    def start_ring(name):
        for sign in (1, -1):
            send_ring(name, 1, sign)

    def take_ring(name, d):
        for sign in (1, -1):
            ring[(id(name[0]), name[1]), d, sign].wait_recv()
            if d < ZN // 2:
                send_ring(name, d + 1, sign)

    def block_at(e, dx, dy):
        return at(dx, e, dy)

    def pick(which, k, j):
        return table[which, k * MAXB + j]

    y_copies, x_copies = {}, {}

    def share_y(e):
        for dx, bufs in ((0, own0), (1, pair0)):
            k = block_at(e, dx, 0)
            for dy in range(1, YN):
                for j in range(MAXB):
                    y_send[e][dy - 1, dx, j] = bufs[e][pick(dy, k, j)]
        y_copies[e] = [
            copy(y_send[e].at[dy - 1], y_got[e].at[YN - dy - 1], (at(0, 0, dy), b)) for dy in range(1, YN)
        ]

    def share_own(e):
        k = block_at(e, 0, 0)
        for j in range(MAXB):
            x_send[e][0, j] = own1[e][pick(4, k, j)]
        x_copies[e] = [copy(x_send[e].at[0], x_got[e].at[0], (at(1, 0, 0), b))]

    def share_column(e):
        for dy in range(1, YN):
            k = block_at(e, 0, dy)
            for j in range(MAXB):
                x_send[e][dy, j] = column1[e][dy - 1, pick(4, k, j)]
        x_copies[e] += [copy(x_send[e].at[pl.ds(1, 3)], x_got[e].at[pl.ds(1, 3)], (at(1, 0, 0), b))]

    def place(lhs, row, k, loads_of):
        names = [jnp.where(j < table[6, k], pick(5, k, j), 8) for j in range(MAXB)]
        for q, load_tile in loads_of:
            tiles = [load_tile(j).astype(jnp.float32) for j in range(MAXB)]
            summed = []
            for i in range(MAXB):
                total = tiles[i]
                for j in range(i + 1, MAXB):
                    total = total + jnp.where(names[i] == names[j], tiles[j], 0.0)
                summed.append(total.astype(jnp.bfloat16))
            here = pl.multiple_of(q * 128 + row, 16)
            for m in range(8):
                value = jnp.zeros((16, TILE), jnp.bfloat16)
                for j in reversed(range(MAXB)):
                    value = jnp.where(names[j] == m, summed[j], value)
                lhs[pl.ds(here, 16), m * TILE : (m + 1) * TILE] = value

    turns = [0, 7, 1, 6, 2, 5, 3, 4]

    def arrived(made):
        for one in made:
            one.wait_recv()

    def near_places(e, lhs, dx, dy):
        row = lax.rem(x + dx, XN) * 64 + lax.rem(y + dy, YN) * 16
        k = block_at(e, dx, dy)
        if dx == 0 and dy == 0:
            loads_of = [(0, lambda j: own0[e][pick(0, k, j)]), (1, lambda j: own1[e][pick(0, k, j)])]
        elif dx == 0:
            loads_of = [
                (0, lambda j: y_got[e][dy - 1, 0, j]),
                (1, lambda j: column1[e][dy - 1, pick(0, k, j)]),
            ]
        elif dy == 0:
            loads_of = [(0, lambda j: pair0[e][pick(0, k, j)]), (1, lambda j: x_got[e][0, j])]
        else:
            loads_of = [(0, lambda j: y_got[e][dy - 1, 1, j]), (1, lambda j: x_got[e][dy, j])]
        return lhs, row, k, loads_of

    def far_last(e, lhs):
        early, late = [], []
        for dx in range(XN):
            for dy in range(YN):
                lhs, row, k, loads_of = near_places(e, lhs, dx, dy)
                early.append((lhs, row, k, loads_of if dx == 0 else loads_of[:1]))
                if dx == 1:
                    late.append((lhs, row, k, loads_of[1:]))
        return early, late

    def places(e, lhs):
        return [near_places(e, lhs, dx, dy) for dx in range(XN) for dy in range(YN)]

    def product(e, lhs, beside=()):
        place_at = turns.index(e) * 128
        share = -(-len(beside) // 2)
        for n in range(2):
            columns = slice(n * 512, (n + 1) * 512)
            got = jnp.dot(lhs[...], bank_v[:, columns], preferred_element_type=jnp.float32)
            got = got.astype(jnp.bfloat16)
            resampled[place_at : place_at + 128, columns] = got[:128]
            resampled[1024 + place_at : 1024 + place_at + 128, columns] = got[128:]
            for item in beside[n * share : (n + 1) * share]:
                place(*item)

    held = lhs_a, lhs_b

    def step(position):
        e, following = turns[position], turns[position + 1]
        arrived(y_copies[following] + x_copies[following])
        product(e, held[position % 2], places(following, held[(position + 1) % 2]))

    def focus(first, last):
        inner = slice(first * 128, last * 128)
        late = slice(1024 + first * 128, 1024 + last * 128)

        for n in range(2):
            columns = slice(n * 512, (n + 1) * 512)
            by_real = jnp.dot(steer_r[:, inner], resampled[inner, columns], preferred_element_type=jnp.float32)
            by_imag = jnp.dot(steer_r[:, inner], resampled[late, columns], preferred_element_type=jnp.float32)
            real, imag = by_real[:64] - by_imag[64:], by_imag[:64] + by_real[64:]
            if first:
                real, imag = real + image[0, :, columns], imag + image[1, :, columns]
            image[0, :, columns] = real
            image[1, :, columns] = imag

    def slices(d):
        return [0] if d == 0 else [4] if d == 4 else [d, ZN - d]

    first_x = copy(own0[0], pair0[0], (at(1, 0, 0), b))
    start_ring(own0_ring)
    first_y = {
        YN - dy - 1: copy(own1[0], column1[0].at[YN - dy - 1], (at(0, 0, dy), b)) for dy in (1, YN - 1)
    }
    start_ring(own1_ring)
    first_y[1] = copy(own1[0], column1[0].at[1], (at(0, 0, 2), b))

    for made in index_loads:
        made.wait()
    near = [w] + [at(0, 0, dy) for dy in range(1, YN)] + [at(1, 0, 0), w, w]
    kind = lax.broadcasted_iota(jnp.int32, (8, wedges), 0)
    lane = lax.broadcasted_iota(jnp.int32, (8, wedges), 1)
    wanted = jnp.zeros((8, wedges), jnp.int32)
    for n, wedge in enumerate(near):
        wanted = jnp.where(kind == n, wedge, wanted)
    chosen = jnp.where(lane == wanted, 1.0, 0.0).astype(jnp.bfloat16)
    across = (((1,), (1,)), ((), ()))

    def choose(ref, rows):
        values = jnp.reshape(ref[...], (rows, wedges)).astype(jnp.float32).astype(jnp.bfloat16)
        return lax.dot_general(chosen, values, across, preferred_element_type=jnp.float32).astype(jnp.int32)

    row = lax.broadcasted_iota(jnp.int32, (8, wedges * MAXB), 0)
    picked = jnp.where(row == 5, choose(ids, wedges * MAXB), choose(offsets, wedges * MAXB))
    table_v[...] = jnp.clip(picked, 0, 7)
    table_v[6:7, 0:wedges] = choose(counts, wedges)[6:7]
    table_load = load(table_v, table, 9)
    first_x.wait_recv()
    start_ring(pair0_ring)
    take_ring(own0_ring, 1)
    for i in (2, 0):
        first_y[i].wait_recv()
        start_ring(column1_rings[i])
    table_load.wait()
    share_own(0)
    share_y(0)
    take_ring(own1_ring, 1)
    for e in slices(1):
        share_own(e)
    first_y[1].wait_recv()
    start_ring(column1_rings[1])
    share_column(0)

    loads[1].wait()
    low_half = lax.broadcasted_iota(jnp.int32, (128, TILE), 1) < 64
    for n, e in enumerate(turns):
        zz = lax.rem(z + e, ZN)
        odd = lax.rem(zz, 2)
        pieces = []
        for xx in range(XN):
            columns = pl.ds(pl.multiple_of((xx * 4 + zz // 2) * TILE, TILE), TILE)
            turn = lax.rem(odd + xx, 2) * 64
            pieces.append(pltpu.roll(steer_v[:, columns].astype(jnp.float32), turn, 1))
        piece = jnp.where(low_half, pieces[0], pieces[1])
        here = slice(n * TILE, (n + 1) * TILE)
        steer_r[:, here] = piece.astype(jnp.bfloat16)
        steer_a[here, :] = jnp.transpose(piece)
        steer_b[here, :] = jnp.transpose(jnp.concatenate([piece[64:], -piece[:64]], axis=0))

    for d in range(1, 5):
        take_ring(pair0_ring, d)
        if d < 4:
            take_ring(own0_ring, d + 1)
        for e in slices(d):
            share_y(e)
        if d >= 3:
            step(2 * d - 5)
        for i in (2, 0):
            take_ring(column1_rings[i], d)
        if d < 4:
            take_ring(own1_ring, d + 1)
            for e in slices(d + 1):
                share_own(e)
        take_ring(column1_rings[1], d)
        for e in slices(d):
            share_column(e)
        if d == 1:
            loads[0].wait()
        if d == 1:
            arrived(y_copies[0] + x_copies[0])
            for item in places(0, held[0]):
                place(*item)
        else:
            step(2 * d - 4)
    focus(0, 5)
    step(5)
    arrived(y_copies[4])
    early, late = far_last(4, held[1])
    product(3, held[0], early)
    focus(5, 7)
    arrived(x_copies[4])
    for item in late:
        place(*item)
    product(4, held[1])
    focus(7, 8)
    stores = [pltpu.make_async_copy(image, focused_out, load_sem.at[2])]
    stores[0].start()

    rows_send[0] = image[:, 0, :]
    rows_send[1] = image[:, 63, :]
    eye = lax.broadcasted_iota(jnp.int32, (128, 128), 0) == lax.broadcasted_iota(jnp.int32, (128, 128), 1)
    for side, column in ((0, 0), (1, 1023)):
        values = jnp.concatenate([image[0, :, column : column + 1], image[1, :, column : column + 1]], axis=0)
        cols_send[side] = jnp.sum(jnp.where(eye, values, 0.0), axis=0, keepdims=True)
    edge = [
        copy(rows_send.at[0], rows_got.at[1], (before, b)),
        copy(rows_send.at[1], rows_got.at[0], (after, b)),
        copy(cols_send.at[0], cols_got.at[1], (w, lax.rem(b + BN - 1, BN))),
        copy(cols_send.at[1], cols_got.at[0], (w, lax.rem(b + 1, BN))),
    ]

    squared = image[0] * image[0] + image[1] * image[1]
    cubed = jnp.concatenate([squared * image[0], squared * image[1]], axis=0).astype(jnp.bfloat16)
    for n in range(4):
        inner = slice(n * 256, (n + 1) * 256)
        late = slice(1024 + n * 256, 1024 + (n + 1) * 256)
        by0 = lax.dot_general(resampled[inner, :], cubed, across, preferred_element_type=jnp.float32)
        by1 = lax.dot_general(resampled[late, :], cubed, across, preferred_element_type=jnp.float32)
        terms = jnp.sum(steer_a[inner, :] * by1 + steer_b[inner, :] * by0, axis=1, keepdims=True)
        for h in range(2):
            part = jnp.where(eye, terms[h * TILE : (h + 1) * TILE], 0.0)
            part_one[2 * n + h] = jnp.sum(part, axis=0, keepdims=True)
    core, half = lax.rem(b, 2), b // 2
    first_group = [(dz, dc) for dc in range(2) for dz in range(ZN) if (dz, dc) != (0, 0)]
    one = []
    for dz, dc in first_group:
        other = first_group.index(((ZN - dz) % ZN, dc))
        one.append(copy(part_one.at[turns.index(dz)], got_one.at[other], (at(0, dz, 0), half * 2 + lax.rem(core + dc, 2))))

    for made in edge:
        made.wait_recv()
    row = lax.broadcasted_iota(jnp.int32, (64, 1024), 0)
    col = lax.broadcasted_iota(jnp.int32, (64, 1024), 1)

    def pull(d0, d1):
        inverse = lax.rsqrt(d0 * d0 + d1 * d1 + EDGE_SOFTNESS)
        return d0 * inverse, d1 * inverse

    f = [image[0], image[1]]
    above = [jnp.where(row == 0, rows_got[0, i : i + 1], pltpu.roll(f[i], 1, 0)) for i in range(2)]
    up = pull(f[0] - above[0], f[1] - above[1])
    below = [jnp.where(row == 63, rows_got[1, i : i + 1], pltpu.roll(f[i], 63, 0)) for i in range(2)]
    down = pull(f[0] - below[0], f[1] - below[1])
    beside = []
    for side in range(2):
        values = jnp.sum(jnp.where(eye, cols_got[side], 0.0), axis=1, keepdims=True)
        beside.append([values[:64], values[64:]])
    left = [jnp.where(col == 0, beside[0][i], pltpu.roll(f[i], 1, 1)) for i in range(2)]
    inward = pull(f[0] - left[0], f[1] - left[1])
    right = [jnp.where(col == 1023, beside[1][i], pltpu.roll(f[i], 1023, 1)) for i in range(2)]
    outward = pull(f[0] - right[0], f[1] - right[1])
    lower = (col > 0) | (b > 0)
    upper = (col < 1023) | (b < BN - 1)
    for i in range(2):
        total = up[i] + down[i] + jnp.where(lower, inward[i], 0.0) + jnp.where(upper, outward[i], 0.0)
        smooth[i] = f[i] - STEP_SIZE * total
    stores.append(pltpu.make_async_copy(smooth, smoothed_out, load_sem.at[3]))
    stores[1].start()

    for made in started:
        made.wait_send()
    for made in one:
        made.wait_recv()
    total = part_one[turns.index(0)]
    for i in range(len(first_group)):
        total = total + got_one[i]
    part_two[...] = total
    second_group = [(dh, dx, dy) for dh in range(2) for dx in range(XN) for dy in range(YN) if (dh, dx, dy) != (0, 0, 0)]
    two = []
    for dh, dx, dy in second_group:
        other = second_group.index((dh, dx, (YN - dy) % YN))
        two.append(copy(part_two, got_two.at[other], (at(dx, 0, dy), lax.rem(half + dh, 2) * 2 + core)))
    for store in stores:
        store.wait()
    for made in two:
        made.wait_send()
    for made in two:
        made.wait_recv()
    row_sum = part_two[...]
    for i in range(len(second_group)):
        row_sum = row_sum + got_two[i]
    offset = x * 64 + y * 16
    turned = pltpu.roll(jnp.broadcast_to(row_sum, (8, TILE)), lax.rem(TILE - offset, TILE), 1)
    gradient_out[...] = turned[0:1, :16] * scale


def hand_on(focused, smoothed, gradient, focused_out, smoothed_out, gradient_out, held, row, sem):
    moves = [
        (src.at[q, pl.ds(h * 32, 32)], held.at[n, q, pl.ds(h * 32, 32)], dst.at[q, pl.ds(h * 32, 32)])
        for n, (src, dst) in enumerate(((focused, focused_out), (smoothed, smoothed_out)))
        for q in range(2)
        for h in range(2)
    ]
    moves.append((gradient, row, gradient_out))
    loads = [pltpu.make_async_copy(src, mid, sem.at[0, n]) for n, (src, mid, _) in enumerate(moves)]
    stores = [pltpu.make_async_copy(mid, dst, sem.at[1, n]) for n, (_, mid, dst) in enumerate(moves)]
    for made in loads:
        made.start()
    for made, store in zip(loads, stores):
        made.wait()
        store.start()
    for made in stores:
        made.wait()


def shards(pulse_data, phase_error, steering, kernel_bank, tile_offsets, kernel_ids, counts):
    bf, f32 = jnp.bfloat16, jnp.float32
    block = pltpu.VMEM((8, 16, TILE), bf)
    scratch = [block] * 24
    scratch += [pltpu.VMEM((3, 8, 16, TILE), bf)] * 8
    scratch += [pltpu.VMEM((3, 2, 4, 16, TILE), bf)] * 16
    scratch += [pltpu.VMEM((4, 4, 16, TILE), bf)] * 16
    scratch += [
        pltpu.VMEM((256, 1024), bf),
        pltpu.VMEM((256, 1024), bf),
        pltpu.VMEM((2048, 1024), bf),
        pltpu.VMEM((1024, 1024), bf),
        pltpu.VMEM((128, 1024), bf),
        pltpu.VMEM((128, 1024), bf),
        pltpu.VMEM((1024, TILE), f32),
        pltpu.VMEM((1024, TILE), f32),
        pltpu.VMEM((2, 64, 1024), f32),
        pltpu.VMEM((2, 64, 1024), f32),
        pltpu.VMEM((2, 2, 1024), f32),
        pltpu.VMEM((2, 2, 1024), f32),
        pltpu.VMEM((2, 1, TILE), f32),
        pltpu.VMEM((2, 1, TILE), f32),
        pltpu.VMEM((8, 1, TILE), f32),
        pltpu.VMEM((15, 1, TILE), f32),
        pltpu.VMEM((1, TILE), f32),
        pltpu.VMEM((15, 1, TILE), f32),
        pltpu.VMEM((64, MAXB, 64), jnp.int32),
        pltpu.VMEM((64, MAXB, 64), jnp.int32),
        pltpu.VMEM((64, 64), jnp.int32),
        pltpu.VMEM((1, 16), f32),
        pltpu.VMEM((2, 16, 1024), bf),
        pltpu.VMEM((8, 256), jnp.int32),
        pltpu.SMEM((8, 256), jnp.int32),
        pltpu.SemaphoreType.DMA((COPIES,)),
        pltpu.SemaphoreType.DMA((COPIES,)),
        pltpu.SemaphoreType.DMA((10,)),
    ]
    scale = math.sqrt(1024 / (4096 * 4096))
    image = jax.ShapeDtypeStruct((2, 64, 1024), f32)
    vmem = pl.BlockSpec(memory_space=pltpu.VMEM)
    anywhere = pl.BlockSpec(memory_space=pl.ANY)
    focused, smoothed, gradient = pl.pallas_call(
        functools.partial(kernel, scale),
        out_shape=(image, image, jax.ShapeDtypeStruct((1, 16), f32)),
        in_specs=[anywhere] * 7,
        out_specs=(anywhere, anywhere, vmem),
        scratch_shapes=scratch,
        compiler_params=pltpu.CompilerParams(
            collective_id=0, has_side_effects=True, vmem_limit_bytes=62 << 20
        ),
    )(
        jnp.transpose(tile_offsets, (0, 2, 1)),
        jnp.transpose(kernel_ids, (0, 2, 1)),
        counts,
        jnp.reshape(phase_error, (1, 16)),
        pulse_data,
        jnp.reshape(steering, (128, 1024)),
        jnp.reshape(kernel_bank, (1024, 1024)),
    )
    results = pl.pallas_call(
        hand_on,
        out_shape=(image, image, jax.ShapeDtypeStruct((1, 16), f32)),
        in_specs=[anywhere] * 3,
        out_specs=[anywhere] * 3,
        scratch_shapes=[pltpu.VMEM((2, 2, 64, 1024), f32), pltpu.VMEM((1, 16), f32), pltpu.SemaphoreType.DMA((2, 9))],
        compiler_params=pltpu.CompilerParams(vmem_limit_bytes=62 << 20),
    )(focused, smoothed, gradient)
    return results[0], results[1], jnp.reshape(results[2], (16,))


def solution(mesh):
    in_specs = (
        P(None, "wedge", "band"),
        P("wedge"),
        P(None, "wedge", None),
        P(None, None, "band"),
        P(),
        P(),
        P(),
    )
    out_specs = (P(None, "wedge", "band"), P(None, "wedge", "band"), P("wedge"))
    return jax.shard_map(shards, mesh=mesh, in_specs=in_specs, out_specs=out_specs, check_vma=False)
```
